128 devices in a mesh: clus: 32 (over z, x, core), grp: 4 (over y).
Axes of the slice: x: 4, y: 4, z: 4, core: 2. Of those that a mesh axis runs over, the one named last changes fastest.
Arguments:
- right_sides: float32 [1024, 16, 256], P(('clus', 'grp')), may hold values from -6 to 6
- diag_shift: float32 [1024, 256], P(('clus', 'grp')), may hold values from 2 to 4
- self_blocks: bfloat16 [1024, 256, 256], P(('clus', 'grp')), may hold values from -0.03125 to 0.03125
- near_blocks: bfloat16 [3072, 256, 256], P(('clus', 'grp')), may hold values from -0.03125 to 0.03125
- far_left: bfloat16 [12288, 32, 256], P(('clus', 'grp')), may hold values from -0.0625 to 0.0625
- far_right: bfloat16 [12288, 32, 256], P(('clus', 'grp')), may hold values from -0.0625 to 0.0625
- far_rank: int32 [12288], P(('clus', 'grp')), may hold values from 8 to 32
- send_leaf: int32 [128, 128, 1], P(('clus', 'grp')), may hold values from 0 to 7, as said below
- block_pos: int32 [2, 15360], P(None, ('clus', 'grp')), may hold values from 0 to 127, as said below
Outputs:
- solution: float32 [1024, 16, 256], P(('clus', 'grp'))
- residual: float32 [1024, 16, 256], P(('clus', 'grp'))
The draws below stay inside these ranges and needn't reach their ends.
Inputs may be any that keep to these rules, and one draw needn't show every extreme that they name: For each sender s and owner o the 1 entries send_leaf[s, o, :] are distinct leaves of s. `block_pos`: each owner's block positions name every one of its 32 * 4 * 1 slot positions at least once.
All inputs are finite; a program needn't handle non-finite values.
Results may differ from the reference program's by a relative error of at most 0.0019.
Values may be sent and summed in bfloat16 or wider, within the bound.
No kernel may reach another device: no remote copies, remote signals or barrier semaphores. Data moves between devices by JAX's collectives and lax.ppermute only.
A program may use at most 64 MiB of HBM per device.

```python
import jax
import jax.numpy as jnp
from jax import lax

LEAF = 256
RANK = 32
RHS = 16
ITERS = 2
LEAF_DEV = 8
SLOT = 1
NEAR_DEV = 24
FAR_DEV = 96
LEAVES = 1024
N_CLUS = 32
N_GRP = 4


def draw_send_leaf(key, part):
    key = jax.random.fold_in(key, 11)
    devices = N_CLUS * N_GRP
    keys = jax.random.split(key, devices * devices)
    orders = jax.vmap(lambda single: jax.random.permutation(single, LEAF_DEV))(keys)
    return orders[:, :SLOT].reshape(devices, devices, SLOT).astype(jnp.int32)


def draw_block_pos(key, part):
    key = jax.random.fold_in(key, 23)
    devices = N_CLUS * N_GRP
    total = devices * SLOT
    per_owner = NEAR_DEV + FAR_DEV
    spare = 2 * per_owner - total

    def one_owner(single):
        first, second, third = jax.random.split(single, 3)
        cover = jax.random.permutation(first, total).astype(jnp.int32)
        extra = jax.random.randint(second, (spare,), 0, total).astype(jnp.int32)
        every = jax.random.permutation(third, jnp.concatenate([cover, extra]))
        return every.reshape(2, per_owner)
    table = jax.vmap(one_owner)(jax.random.split(key, devices))
    return jnp.transpose(table, (1, 0, 2)).reshape(2, devices * per_owner).astype(jnp.int32)


def set_ends(values, own_key, smallest, high):
    spot = [jax.random.randint(jax.random.fold_in(own_key, axis), (), 0, length) for axis, length in enumerate(values.shape)]
    main_axis = values.shape.index(max(values.shape))
    next_to = spot[:main_axis] + [(spot[main_axis] + 1) % values.shape[main_axis]] + spot[main_axis + 1:]
    return values.at[tuple(spot)].set(smallest).at[tuple(next_to)].set(high)


def level_of(stream_key, dims, shards, least, high):
    def one(axis_at, parts):
        steps = jax.random.uniform(jax.random.fold_in(jax.random.fold_in(stream_key, 6), axis_at), (parts,), jnp.float32, least / len(shards), high / len(shards))
        return jnp.repeat(jnp.exp(steps), dims[axis_at] // parts).reshape((-1,) + (1,) * (len(dims) - axis_at - 1))

    loudness = one(*shards[0])
    for cut in shards[1:]:
        loudness = loudness * one(*cut)
    return loudness


def normal_values(stream_key, extent, deviation, most, cuts=(), kind=jnp.bfloat16):
    array = deviation * jax.random.normal(stream_key, extent, jnp.float32)
    if cuts:
        array = array * level_of(stream_key, extent, cuts, -0.22, 0.18)
    return jnp.clip(array, -most, most).astype(kind)


def setup_inputs(seed: int = 0) -> dict:
    seeds = jax.random.split(jax.random.key(seed), 10)
    return {
        "right_sides": normal_values(seeds[0], (LEAVES, RHS, LEAF), 1.0, 6.0, ((0, 128),), jnp.float32),
        "diag_shift": jnp.clip(2.0 + 2.0 * jax.random.uniform(seeds[1], (LEAVES, LEAF), jnp.float32) ** level_of(seeds[1], (LEAVES, LEAF), ((0, 128),), -0.2, 0.2), 2.0, 4.0),
        "self_blocks": normal_values(seeds[2], (LEAVES, LEAF, LEAF), (0.08 / LEAF ** 0.5), 0.03125, ((0, 128),)),
        "near_blocks": normal_values(seeds[3], (N_CLUS * N_GRP * NEAR_DEV, LEAF, LEAF), (0.08 / LEAF ** 0.5), 0.03125, ((0, 128),)),
        "far_left": normal_values(seeds[4], (N_CLUS * N_GRP * FAR_DEV, RANK, LEAF), (0.16 / LEAF ** 0.5), 0.0625, ((0, 128),)),
        "far_right": normal_values(seeds[5], (N_CLUS * N_GRP * FAR_DEV, RANK, LEAF), (0.16 / LEAF ** 0.5), 0.0625, ((0, 128),)),
        "far_rank": set_ends(jax.random.randint(seeds[6], (N_CLUS * N_GRP * FAR_DEV,), RANK // 4, RANK + 1), jax.random.fold_in(seeds[6], 1), RANK // 4, RANK).astype(jnp.int32),
        "send_leaf": draw_send_leaf(jax.random.fold_in(seeds[9], 71), 0),
        "block_pos": draw_block_pos(jax.random.fold_in(seeds[9], 71), 0),
    }


def inner_gram(left_field, right_field):
    return jnp.einsum('lri,lsi->rs', left_field, right_field, precision=lax.Precision.HIGHEST)

def combine_cols(field, coefs):
    return jnp.einsum('lri,rs->lsi', field, coefs, precision=lax.Precision.HIGHEST)

def small_solve(matrix, target):
    factor = jnp.linalg.cholesky(matrix)
    return jax.scipy.linalg.cho_solve((factor, True), target)

def to_half(values):
    return lax.optimization_barrier(values.astype(jnp.bfloat16)).astype(jnp.float32)

def reference(right_sides, diag_shift, self_blocks, near_blocks, far_left, far_right, far_rank, send_leaf, block_pos):
    devices = N_CLUS * N_GRP
    per_owner = NEAR_DEV + FAR_DEV
    sources = jnp.arange(devices, dtype=jnp.int32)[:, None, None] * LEAF_DEV + send_leaf.astype(jnp.int32)
    leaf_of = jnp.transpose(sources, (1, 0, 2)).reshape(devices, devices * SLOT)
    positions = block_pos.astype(jnp.int32).reshape(2, devices, per_owner)
    row_ids = jnp.take_along_axis(leaf_of, positions[0], axis=1).astype(jnp.int32)
    col_ids = jnp.take_along_axis(leaf_of, positions[1], axis=1).astype(jnp.int32)
    near_all = near_blocks.reshape(devices, NEAR_DEV, LEAF, LEAF)
    left_all = far_left.reshape(devices, FAR_DEV, RANK, LEAF)
    right_all = far_right.reshape(devices, FAR_DEV, RANK, LEAF)
    rank_mask = (jnp.arange(RANK, dtype=jnp.int32)[None, None, :] < far_rank.astype(jnp.int32).reshape(devices, FAR_DEV)[:, :, None]).astype(jnp.float32)
    selfs = self_blocks.astype(jnp.float32)

    def operate(direction):
        halved = to_half(direction)
        base = diag_shift[:, None, :] * direction
        base = base + jnp.einsum('lij,lrj->lri', selfs, halved) + jnp.einsum('lij,lri->lrj', selfs, halved)

        def owner(total, pieces):
            near_o, left_o, right_o, mask_o, rows_o, cols_o = pieces
            x_row = halved[rows_o]
            x_col = halved[cols_o]
            near_f = near_o.astype(jnp.float32)
            left_f = left_o.astype(jnp.float32)
            right_f = right_o.astype(jnp.float32)
            rows_near = jnp.einsum('bij,brj->bri', near_f, x_col[:NEAR_DEV])
            cols_near = jnp.einsum('bij,bri->brj', near_f, x_row[:NEAR_DEV])
            right_proj = to_half(jnp.einsum('bkj,brj->bkr', right_f, x_col[NEAR_DEV:]) * mask_o[:, :, None])
            left_proj = to_half(jnp.einsum('bki,bri->bkr', left_f, x_row[NEAR_DEV:]) * mask_o[:, :, None])
            rows_far = jnp.einsum('bki,bkr->bri', left_f, right_proj)
            cols_far = jnp.einsum('bkj,bkr->brj', right_f, left_proj)
            total = total + jax.ops.segment_sum(jnp.concatenate([rows_near, rows_far], axis=0), rows_o, num_segments=LEAVES)
            total = total + jax.ops.segment_sum(jnp.concatenate([cols_near, cols_far], axis=0), cols_o, num_segments=LEAVES)
            return (total, None)
        total, _ = lax.scan(owner, jnp.zeros_like(direction), (near_all, left_all, right_all, rank_mask, row_ids, col_ids))
        return base + total
    solution = jnp.zeros_like(right_sides)
    residual = right_sides
    direction = right_sides
    res_gram = inner_gram(residual, residual)
    for iteration in range(ITERS):
        product = operate(direction)
        step_coef = small_solve(inner_gram(direction, product), res_gram)
        solution = solution + combine_cols(direction, step_coef)
        residual = residual - combine_cols(product, step_coef)
        if iteration + 1 < ITERS:
            next_gram = inner_gram(residual, residual)
            dir_coef = small_solve(res_gram, next_gram)
            direction = residual + combine_cols(direction, dir_coef)
            res_gram = next_gram
    return (solution, residual)
```

```python
import jax
import jax.numpy as jnp
from jax import lax
from jax.experimental import pallas as pl
from jax.experimental.pallas import tpu as pltpu
from jax.sharding import PartitionSpec as P

AXES = ("clus", "grp")
HIGHEST = lax.Precision.HIGHEST
NT = (((1,), (1,)), ((), ()))
F32 = jnp.float32
BF16 = jnp.bfloat16

VMEM = pl.BlockSpec(memory_space=pltpu.VMEM)
SMEM = pl.BlockSpec(memory_space=pltpu.SMEM)


def iota(shape, dim):
    return lax.broadcasted_iota(jnp.int32, shape, dim)


def spread(values):
    values = values + pltpu.roll(values, 64, 1)
    values = values + pltpu.roll(values, 32, 1)
    return values + pltpu.roll(values, 16, 1)


def block_mask():
    return iota((128, 128), 0) // 16 == iota((128, 128), 1) // 16


def fold(products):
    kept = jnp.where(block_mask(), products, 0.0)
    total = kept[0:16]
    for part in range(1, 8):
        total = total + kept[16 * part : 16 * part + 16]
    return spread(total)


def kron_rows(coefs):
    tiled = jnp.concatenate([coefs] * 8, axis=0)
    return jnp.where(block_mask(), tiled, 0.0).T


def combine(field, kron):
    return jnp.dot(kron, field, precision=HIGHEST, preferred_element_type=F32)


def gram(left, right):
    return fold(lax.dot_general(left, right, NT, precision=HIGHEST, preferred_element_type=F32))


def solve(matrix, target):
    group = iota((16, 128), 1) // 16
    row_at = iota((16, 128), 0)
    work = jnp.where(group == 0, matrix, target)
    for step in range(16):
        column = jnp.broadcast_to(work[:, step : step + 1], (16, 128))
        pivot = column[step : step + 1, :]
        scaled = work[step : step + 1, :] * jnp.where(pivot > 0, 1.0 / pivot, jnp.nan)
        work = jnp.where(row_at == step, scaled, work - column * scaled)
    return jnp.where(group == 0, pltpu.roll(work, 16, 1), work)


def pack(first, second):
    group = iota((8, 128), 1) // 16
    tile = jnp.zeros((8, 128), F32)
    at = 0
    for matrix in (first, second):
        high = matrix.astype(BF16).astype(F32)
        low = matrix - high
        for piece in (high, low):
            for half in (piece[0:8], piece[8:16]):
                tile = jnp.where(group == at, half, tile)
                at += 1
    return tile.astype(BF16)


def unpack(tile):
    group = iota((8, 128), 1) // 16
    joined = tile + pltpu.roll(tile, 128 - 32, 1)
    halves = [spread(jnp.where(group == at, joined, 0.0)) for at in (0, 1, 4, 5)]
    return jnp.concatenate(halves[0:2], axis=0), jnp.concatenate(halves[2:4], axis=0)


def send_kernel(leaf_ref, field_ref, message_ref, half_ref):
    half_ref[...] = field_ref[...].astype(BF16)

    def some(at, carry):
        for part in range(8):
            owner = at * 8 + part
            message_ref[owner] = half_ref[leaf_ref[owner]]
        return carry

    lax.fori_loop(0, message_ref.shape[0] // 8, some, 0)


def base_kernel(field_ref, shift_ref, self_ref, base_ref, curve_ref, norm_ref):
    leaves = field_ref.shape[0]
    for leaf in range(leaves):
        field = field_ref[leaf]
        half = field.astype(BF16)
        block = self_ref[leaf]
        total = shift_ref[leaf : leaf + 1, :] * field
        total = total + lax.dot_general(half, block, NT, preferred_element_type=F32)
        base_ref[leaf] = total + jnp.dot(half, block, preferred_element_type=F32)
    fields = field_ref[...].reshape(128, 256)
    curve_ref[...] = gram(fields, base_ref[...].reshape(128, 256))
    norm_ref[...] = gram(fields, fields)


def owner_kernel(
    rank_ref, at_ref, x_ref, near_ref, left_ref, right_ref, curve_ref, norm_ref, out_ref, acc_ref
):
    slots = x_ref.shape[0]
    near = near_ref.shape[0]
    far = left_ref.shape[0]

    def clear(at, carry):
        acc_ref[pl.ds(at * 8, 8)] = jnp.zeros((8, 16, 256), F32)
        return carry

    lax.fori_loop(0, slots // 8, clear, 0)

    def near_some(at, carry):
        sums = []
        for part in range(4):
            which = at * 4 + part
            row, col = at_ref[0, which], at_ref[1, which]
            block = near_ref[which]
            sums.append(
                (row, lax.dot_general(x_ref[col], block, NT, preferred_element_type=F32))
            )
            sums.append((col, jnp.dot(x_ref[row], block, preferred_element_type=F32)))
        for slot, value in sums:
            acc_ref[slot] += value
        return carry

    lax.fori_loop(0, near // 4, near_some, 0)

    lane = iota((16, 256), 1)

    def far_some(at, carry):
        first = at * 8
        left = left_ref[pl.ds(first, 8)].reshape(256, 256)
        right = right_ref[pl.ds(first, 8)].reshape(256, 256)
        rows = [at_ref[0, near + first + part] for part in range(8)]
        cols = [at_ref[1, near + first + part] for part in range(8)]
        x_row = jnp.concatenate([x_ref[slot] for slot in rows], axis=0)
        x_col = jnp.concatenate([x_ref[slot] for slot in cols], axis=0)
        kept = jnp.concatenate(
            [
                (lane >= 32 * part) & (lane < 32 * part + rank_ref[first + part])
                for part in range(8)
            ],
            axis=0,
        )
        right_proj = lax.dot_general(x_col, right, NT, preferred_element_type=F32)
        left_proj = lax.dot_general(x_row, left, NT, preferred_element_type=F32)
        right_proj = jnp.where(kept, right_proj, 0.0).astype(BF16)
        left_proj = jnp.where(kept, left_proj, 0.0).astype(BF16)
        to_row = jnp.dot(right_proj, left, preferred_element_type=F32)
        to_col = jnp.dot(left_proj, right, preferred_element_type=F32)
        for part in range(8):
            acc_ref[rows[part]] += to_row[16 * part : 16 * part + 16]
            acc_ref[cols[part]] += to_col[16 * part : 16 * part + 16]
        return carry

    lax.fori_loop(0, far // 8, far_some, 0)

    def finish(at, products):
        here = pl.ds(at * 8, 8)
        sums = acc_ref[here].astype(BF16)
        out_ref[here, 0:16, :] = sums[:, :, 0:128]
        out_ref[here, 16:32, :] = sums[:, :, 128:256]
        return products + lax.dot_general(
            x_ref[here].reshape(128, 256),
            sums.reshape(128, 256),
            NT,
            preferred_element_type=F32,
        )

    products = lax.fori_loop(0, slots // 8, finish, jnp.zeros((128, 128), F32))
    tile = pack(fold(products) + curve_ref[...], norm_ref[...])

    def attach(at, carry):
        out_ref[pl.ds(at * 8, 8), 32:40, :] = jnp.broadcast_to(tile[None], (8, 8, 128))
        return carry

    lax.fori_loop(0, slots // 8, attach, 0)


def add_returned(leaf_ref, sums_ref, acc_ref):
    def some(at, tiles):
        for part in range(8):
            owner = at * 8 + part
            leaf = leaf_ref[owner]
            acc_ref[leaf, :, 0:128] += sums_ref[owner, 0:16, :].astype(F32)
            acc_ref[leaf, :, 128:256] += sums_ref[owner, 16:32, :].astype(F32)
            tiles = tiles + sums_ref[owner, 32:40, :].astype(F32)
        return tiles

    return lax.fori_loop(0, sums_ref.shape[0] // 8, some, jnp.zeros((8, 128), F32))


def leaf_kernel(
    leaf_ref, sums_ref, base_ref, field_ref,
    residual_ref, image_ref, message_ref, curve_ref, norm_ref, step_ref, half_ref,
):
    image_ref[...] = base_ref[...]
    curve, norm = unpack(add_returned(leaf_ref, sums_ref, image_ref))
    step = solve(curve, norm)
    curve_ref[...] = curve
    norm_ref[...] = norm
    step_ref[...] = step
    image = image_ref[...].reshape(128, 256)
    residual = field_ref[...].reshape(128, 256) - combine(image, kron_rows(step))
    residual_ref[...] = residual.reshape(residual_ref.shape)
    half_ref[...] = residual.reshape(residual_ref.shape).astype(BF16)

    def some(at, carry):
        for part in range(8):
            owner = at * 8 + part
            message_ref[owner] = half_ref[leaf_ref[owner]]
        return carry

    lax.fori_loop(0, message_ref.shape[0] // 8, some, 0)


def final_kernel(
    leaf_ref, sums_ref, base_ref, field_ref, residual_ref, image_ref,
    curve_ref, norm_ref, step_ref, solution_ref, out_ref, acc_ref,
):
    acc_ref[...] = base_ref[...]
    curve, next_norm = unpack(add_returned(leaf_ref, sums_ref, acc_ref))
    coef = solve(norm_ref[...], next_norm)
    narrow = coef[:, 0:16]
    moved = jnp.dot(curve_ref[:, 0:16], coef, precision=HIGHEST, preferred_element_type=F32)
    moved = lax.dot_general(
        narrow, moved, (((0,), (0,)), ((), ())), precision=HIGHEST, preferred_element_type=F32
    )
    step = solve(curve - moved, next_norm)
    kron_step = kron_rows(step)
    kron_coef = kron_rows(coef)
    field = field_ref[...].reshape(128, 256)
    residual = residual_ref[...].reshape(128, 256)
    direction = residual + combine(field, kron_coef)
    product = acc_ref[...].reshape(128, 256) + combine(
        image_ref[...].reshape(128, 256), kron_coef
    )
    answer = combine(field, kron_rows(step_ref[...])) + combine(direction, kron_step)
    solution_ref[...] = answer.reshape(solution_ref.shape)
    out_ref[...] = (residual - combine(product, kron_step)).reshape(out_ref.shape)


def call(kernel, ins, outs, scratch=(), cost=None):
    return pl.pallas_call(
        kernel,
        out_shape=[jax.ShapeDtypeStruct(shape, kind) for shape, kind in outs],
        in_specs=list(ins),
        out_specs=[VMEM] * len(outs),
        scratch_shapes=[pltpu.VMEM(shape, kind) for shape, kind in scratch],
        compiler_params=pltpu.CompilerParams(vmem_limit_bytes=32 * 1024 * 1024),
        cost_estimate=cost,
    )


def swap(values):
    return lax.all_to_all(values, AXES, split_axis=0, concat_axis=0, tiled=True)


def shards(
    right_sides,
    diag_shift,
    self_blocks,
    near_blocks,
    far_left,
    far_right,
    far_rank,
    send_leaf,
    block_pos,
):
    leaves, rhs, size = right_sides.shape
    slots = send_leaf.shape[1]
    targets = send_leaf.reshape(slots)
    whole = ((leaves, rhs, size), F32)
    small = ((rhs, 128), F32)
    message = ((slots, rhs, size), BF16)
    returned = ((slots, 40, 128), BF16)
    local_cost = pl.CostEstimate(
        flops=4 * leaves * rhs * size * size, bytes_accessed=2 * leaves * size * size, transcendentals=0
    )
    send = call(send_kernel, [SMEM, VMEM], [message], [((leaves, rhs, size), BF16)])
    base = call(base_kernel, [VMEM] * 3, [whole, small, small], cost=local_cost)
    owner = call(
        owner_kernel, [SMEM, SMEM] + [VMEM] * 6, [returned], [((slots, rhs, size), F32)]
    )
    leaf = call(
        leaf_kernel,
        [SMEM] + [VMEM] * 3,
        [whole, whole, message, small, small, small],
        [((leaves, rhs, size), BF16)],
    )
    final = call(final_kernel, [SMEM] + [VMEM] * 8, [whole, whole], [whole])

    with jax.named_scope("send"):
        (outgoing,) = send(targets, right_sides)
    incoming = swap(outgoing)
    with jax.named_scope("base"):
        base_image, curve, norm = base(right_sides, diag_shift, self_blocks)
    with jax.named_scope("owner"):
        (sums,) = owner(
            far_rank, block_pos, incoming, near_blocks, far_left, far_right, curve, norm
        )
    back = swap(sums)
    with jax.named_scope("leaf"):
        residual, image, outgoing, curve, norm, step = leaf(
            targets, back, base_image, right_sides
        )
    incoming = swap(outgoing)
    with jax.named_scope("base"):
        base_image, next_curve, next_norm = base(residual, diag_shift, self_blocks)
    with jax.named_scope("owner"):
        (sums,) = owner(
            far_rank, block_pos, incoming, near_blocks, far_left, far_right, next_curve, next_norm
        )
    back = swap(sums)
    with jax.named_scope("final"):
        answer, residual = final(
            targets, back, base_image, right_sides, residual, image, curve, norm, step
        )
    return (answer, residual)


def solution(mesh):
    split = P(AXES, None, None)
    placed = (
        split,
        P(AXES, None),
        split,
        split,
        split,
        split,
        P(AXES),
        split,
        P(None, AXES),
    )
    return jax.shard_map(
        shards, mesh=mesh, in_specs=placed, out_specs=(split, split), check_vma=False
    )
```

```python
import jax
import jax.numpy as jnp
from jax import lax
from jax.experimental import pallas as pl
from jax.experimental.pallas import tpu as pltpu
from jax.sharding import PartitionSpec as P

AXES = ("clus", "grp")
HIGHEST = lax.Precision.HIGHEST
NT = (((1,), (1,)), ((), ()))
F32 = jnp.float32
BF16 = jnp.bfloat16

VMEM = pl.BlockSpec(memory_space=pltpu.VMEM)
HBM = pl.BlockSpec(memory_space=pltpu.HBM)
KEPT = pl.BlockSpec(memory_space=pltpu.VMEM)


def iota(shape, dim):
    return lax.broadcasted_iota(jnp.int32, shape, dim)


def spread(values):
    values = values + pltpu.roll(values, 64, 1)
    values = values + pltpu.roll(values, 32, 1)
    return values + pltpu.roll(values, 16, 1)


def block_mask():
    return iota((128, 128), 0) // 16 == iota((128, 128), 1) // 16


def fold(products):
    kept = jnp.where(block_mask(), products, 0.0)
    total = kept[0:16]
    for part in range(1, 8):
        total = total + kept[16 * part : 16 * part + 16]
    return spread(total)


def kron_rows(coefs):
    tiled = jnp.concatenate([coefs] * 8, axis=0)
    return jnp.where(block_mask(), tiled, 0.0).T


def combine(field, kron):
    return jnp.dot(kron, field, precision=HIGHEST, preferred_element_type=F32)


def gram(left, right):
    return fold(lax.dot_general(left, right, NT, precision=HIGHEST, preferred_element_type=F32))


def columns(matrix):
    return [jnp.broadcast_to(matrix[:, at : at + 1], (16, 128)) for at in range(16)]


def factor(matrix):
    row_at = iota((16, 128), 0)
    left = columns(matrix)
    steps = []
    for step in range(16):
        column = left[step]
        pivot = column[step : step + 1]
        scale = jnp.where(pivot > 0, 1.0 / pivot, jnp.nan)
        steps.append((column, scale))
        for later in range(step + 1, 16):
            scaled = left[later][step : step + 1] * scale
            left[later] = jnp.where(row_at == step, scaled, left[later] - column * scaled)
    return steps


def apply_factor(steps, target):
    row_at = iota((16, 128), 0)
    for step, (column, scale) in enumerate(steps):
        scaled = target[step : step + 1] * scale
        target = jnp.where(row_at == step, scaled, target - column * scaled)
    return target


def solve(matrix, target):
    return apply_factor(factor(matrix), target)


def product(left, right):
    total = left[0] * right[0:1]
    for at in range(1, 16):
        total = total + left[at] * right[at : at + 1]
    return total


def pack(first, second):
    group = iota((8, 128), 1) // 16
    tile = jnp.zeros((8, 128), F32)
    at = 0
    for matrix in (first, second):
        high = matrix.astype(BF16).astype(F32)
        low = matrix - high
        for piece in (high, low):
            for half in (piece[0:8], piece[8:16]):
                tile = jnp.where(group == at, half, tile)
                at += 1
    return tile.astype(BF16)


def unpack(tile):
    group = iota((8, 128), 1) // 16
    joined = tile + pltpu.roll(tile, 128 - 32, 1)
    halves = [spread(jnp.where(group == at, joined, 0.0)) for at in (0, 1, 4, 5)]
    return jnp.concatenate(halves[0:2], axis=0), jnp.concatenate(halves[2:4], axis=0)


def fill(leaf_ref, half_ref, stage_ref, message_ref, sems):
    part = stage_ref.shape[0] // 4
    copies = []
    for quarter in range(4):

        def some(at, carry, first=quarter * part):
            for inner in range(8):
                owner = first + at * 8 + inner
                stage_ref[owner] = half_ref[leaf_ref[owner]]
            return carry

        lax.fori_loop(0, part // 8, some, 0)
        here = pl.ds(quarter * part, part)
        copy = pltpu.make_async_copy(stage_ref.at[here], message_ref.at[here], sems.at[quarter])
        copy.start()
        copies.append(copy)
    return copies


def send_kernel(leaf_hbm, field_hbm, message_ref, leaf_ref, field_ref, half_ref, stage_ref, sems):
    leaf_copy = pltpu.make_async_copy(leaf_hbm, leaf_ref, sems.at[4])
    field_copy = pltpu.make_async_copy(field_hbm, field_ref, sems.at[5])
    leaf_copy.start()
    field_copy.start()
    field_copy.wait()
    half_ref[...] = field_ref[...].astype(BF16)
    leaf_copy.wait()
    for copy in fill(leaf_ref, half_ref, stage_ref, message_ref, sems):
        copy.wait()


def local_product(field_ref, shift_ref, self_ref, base_ref, small_ref):
    for leaf in range(field_ref.shape[0]):
        field = field_ref[leaf]
        half = field.astype(BF16)
        block = self_ref[leaf]
        total = shift_ref[leaf : leaf + 1, :] * field
        total = total + lax.dot_general(half, block, NT, preferred_element_type=F32)
        base_ref[leaf] = total + jnp.dot(half, block, preferred_element_type=F32)
    fields = field_ref[...].reshape(128, 256)
    small_ref[0] = gram(fields, base_ref[...].reshape(128, 256))
    small_ref[1] = gram(fields, fields)


def base_kernel(
    field_ref, shift_ref, self_ref, near_hbm, left_hbm, right_hbm,
    base_ref, small_ref, near_ref, left_ref, right_ref, sems,
):
    copies = [
        pltpu.make_async_copy(near_hbm, near_ref, sems.at[0]),
        pltpu.make_async_copy(left_hbm, left_ref, sems.at[1]),
        pltpu.make_async_copy(right_hbm, right_ref, sems.at[2]),
    ]
    for copy in copies:
        copy.start()
    local_product(field_ref, shift_ref, self_ref, base_ref, small_ref)
    for copy in copies:
        copy.wait()


def next_base_kernel(
    field_ref, shift_ref, self_ref, old_ref, first_ref, base_ref, small_ref, part_ref, steps_ref
):
    local_product(field_ref, shift_ref, self_ref, base_ref, small_ref)
    part = combine(first_ref[...].reshape(128, 256), kron_rows(old_ref[2]))
    part_ref[...] = part.reshape(part_ref.shape)
    for step, (column, scale) in enumerate(factor(old_ref[1])):
        steps_ref[step] = column
        steps_ref[16, step : step + 1] = scale


def owner_kernel(
    rank_hbm, at_hbm, x_hbm, near_ref, left_ref, right_ref, small_ref,
    out_ref, rank_ref, at_ref, x_ref, acc_ref, sems,
):
    copies = [
        pltpu.make_async_copy(at_hbm, at_ref, sems.at[0]),
        pltpu.make_async_copy(x_hbm, x_ref, sems.at[1]),
        pltpu.make_async_copy(rank_hbm, rank_ref, sems.at[2]),
    ]
    for copy in copies:
        copy.start()
    slots = x_ref.shape[0]
    near = near_ref.shape[0]
    far = left_ref.shape[0]

    def clear(at, carry):
        acc_ref[pl.ds(at * 8, 8)] = jnp.zeros((8, 16, 256), F32)
        return carry

    lax.fori_loop(0, slots // 8, clear, 0)
    for copy in copies:
        copy.wait()

    def near_some(at, carry):
        sums = []
        for part in range(8):
            which = at * 8 + part
            row, col = at_ref[0, which], at_ref[1, which]
            block = near_ref[which]
            sums.append(
                (row, lax.dot_general(x_ref[col], block, NT, preferred_element_type=F32))
            )
            sums.append((col, jnp.dot(x_ref[row], block, preferred_element_type=F32)))
        for slot, value in sums:
            acc_ref[slot] += value
        return carry

    lax.fori_loop(0, near // 8, near_some, 0)

    lane = iota((16, 256), 1)

    def far_project(first):
        left = left_ref[pl.ds(first, 8)].reshape(256, 256)
        right = right_ref[pl.ds(first, 8)].reshape(256, 256)
        rows = [at_ref[0, near + first + part] for part in range(8)]
        cols = [at_ref[1, near + first + part] for part in range(8)]
        x_row = jnp.concatenate([x_ref[slot] for slot in rows], axis=0)
        x_col = jnp.concatenate([x_ref[slot] for slot in cols], axis=0)
        kept = jnp.concatenate(
            [
                (lane >= 32 * part) & (lane < 32 * part + rank_ref[first + part])
                for part in range(8)
            ],
            axis=0,
        )
        right_proj = lax.dot_general(x_col, right, NT, preferred_element_type=F32)
        left_proj = lax.dot_general(x_row, left, NT, preferred_element_type=F32)
        right_proj = jnp.where(kept, right_proj, 0.0).astype(BF16)
        left_proj = jnp.where(kept, left_proj, 0.0).astype(BF16)
        return rows, cols, left, right, right_proj, left_proj

    def far_some(at, carry):
        sums = []
        for rows, cols, left, right, right_proj, left_proj in [
            far_project(at * 32 + 8 * group) for group in range(4)
        ]:
            to_row = jnp.dot(right_proj, left, preferred_element_type=F32)
            to_col = jnp.dot(left_proj, right, preferred_element_type=F32)
            for part in range(8):
                sums.append((rows[part], to_row[16 * part : 16 * part + 16]))
                sums.append((cols[part], to_col[16 * part : 16 * part + 16]))
        for slot, value in sums:
            acc_ref[slot] += value
        return carry

    lax.fori_loop(0, far // 32, far_some, 0)

    products = jnp.zeros((128, 128), F32)
    for at in range(slots // 8):
        here = slice(at * 8, at * 8 + 8)
        sums = acc_ref[here].astype(BF16)
        out_ref[here, 0:16, :] = sums[:, :, 0:128]
        out_ref[here, 16:32, :] = sums[:, :, 128:256]
        products = products + lax.dot_general(
            x_ref[here].reshape(128, 256),
            sums.reshape(128, 256),
            NT,
            preferred_element_type=F32,
        )
    tile = pack(fold(products) + small_ref[0], small_ref[1])

    def attach(at, carry):
        out_ref[pl.ds(at * 8, 8), 32:40, :] = jnp.broadcast_to(tile[None], (8, 8, 128))
        return carry

    lax.fori_loop(0, slots // 8, attach, 0)


def add_returned(leaf_ref, sums_ref, acc_ref):
    def some(at, tiles):
        for part in range(8):
            owner = at * 8 + part
            leaf = leaf_ref[owner]
            acc_ref[leaf, :, 0:128] += sums_ref[owner, 0:16, :].astype(F32)
            acc_ref[leaf, :, 128:256] += sums_ref[owner, 16:32, :].astype(F32)
            tiles = tiles + sums_ref[owner, 32:40, :].astype(F32)
        return tiles

    return lax.fori_loop(0, sums_ref.shape[0] // 8, some, jnp.zeros((8, 128), F32))


def leaf_kernel(
    leaf_hbm, sums_ref, base_ref, field_ref,
    residual_ref, image_ref, small_ref, message_ref,
    leaf_ref, half_ref, stage_ref, sems,
):
    leaf_copy = pltpu.make_async_copy(leaf_hbm, leaf_ref, sems.at[4])
    leaf_copy.start()
    image_ref[...] = base_ref[...]
    leaf_copy.wait()
    curve, norm = unpack(add_returned(leaf_ref, sums_ref, image_ref))
    step = solve(curve, norm)
    image = image_ref[...].reshape(128, 256)
    residual = field_ref[...].reshape(128, 256) - combine(image, kron_rows(step))
    half_ref[...] = residual.reshape(residual_ref.shape).astype(BF16)
    copies = fill(leaf_ref, half_ref, stage_ref, message_ref, sems)
    residual_ref[...] = residual.reshape(residual_ref.shape)
    small_ref[0] = curve
    small_ref[1] = norm
    small_ref[2] = step
    for copy in copies:
        copy.wait()


def final_kernel(
    leaf_hbm, sums_ref, base_ref, field_ref, residual_ref, image_ref, small_ref, part_ref, steps_ref,
    solution_ref, out_ref, leaf_ref, acc_ref, sem,
):
    leaf_copy = pltpu.make_async_copy(leaf_hbm, leaf_ref, sem)
    leaf_copy.start()
    acc_ref[...] = base_ref[...]
    leaf_copy.wait()
    curve, next_norm = unpack(add_returned(leaf_ref, sums_ref, acc_ref))
    steps = [(steps_ref[step], steps_ref[16, step : step + 1]) for step in range(16)]
    coef = apply_factor(steps, next_norm)
    moved = product(columns(small_ref[0]), coef)
    moved = product(columns(coef.T[0:16]), moved)
    step = solve(curve - moved, next_norm)
    kron_coef = kron_rows(coef)
    residual = residual_ref[...].reshape(128, 256)
    direction = residual + combine(field_ref[...].reshape(128, 256), kron_coef)
    image = acc_ref[...].reshape(128, 256) + combine(
        image_ref[...].reshape(128, 256), kron_coef
    )
    kron_step = kron_rows(step)
    answer = part_ref[...].reshape(128, 256) + combine(direction, kron_step)
    solution_ref[...] = answer.reshape(solution_ref.shape)
    out_ref[...] = (residual - combine(image, kron_step)).reshape(out_ref.shape)


def call(kernel, ins, outs, scratch, cost=None):
    spaces = [HBM if getattr(out, "memory_space", None) == pltpu.HBM else VMEM for out in outs]
    run = pl.pallas_call(
        kernel,
        out_shape=list(outs),
        in_specs=list(ins),
        out_specs=spaces,
        scratch_shapes=list(scratch),
        compiler_params=pltpu.CompilerParams(vmem_limit_bytes=24 * 1024 * 1024),
        cost_estimate=cost,
    )

    def placed(*values):
        return run(
            *(
                pltpu.with_memory_space_constraint(value, spec.memory_space)
                if spec is HBM or spec is KEPT
                else value
                for value, spec in zip(values, ins)
            )
        )

    return placed


def swap(values):
    return lax.all_to_all(values, AXES, split_axis=0, concat_axis=0, tiled=True)


def shards(
    right_sides,
    diag_shift,
    self_blocks,
    near_blocks,
    far_left,
    far_right,
    far_rank,
    send_leaf,
    block_pos,
):
    leaves, rhs, size = right_sides.shape
    slots = send_leaf.shape[1]
    targets = send_leaf.reshape(slots)
    whole = (leaves, rhs, size)
    message = (slots, rhs, size)
    local_cost = pl.CostEstimate(
        flops=4 * leaves * rhs * size * size, bytes_accessed=2 * leaves * size * size, transcendentals=0
    )
    send = call(
        send_kernel,
        [HBM, HBM],
        [pltpu.HBM(message, BF16)],
        [
            pltpu.SMEM((slots,), jnp.int32),
            pltpu.VMEM(whole, F32),
            pltpu.VMEM(whole, BF16),
            pltpu.VMEM(message, BF16),
            pltpu.SemaphoreType.DMA((6,)),
        ],
    )
    base = call(
        base_kernel,
        [VMEM, VMEM, VMEM, HBM, HBM, HBM],
        [
            pltpu.VMEM(whole, F32),
            pltpu.VMEM((2, rhs, 128), F32),
            pltpu.VMEM(near_blocks.shape, BF16),
            pltpu.VMEM(far_left.shape, BF16),
            pltpu.VMEM(far_right.shape, BF16),
        ],
        [pltpu.SemaphoreType.DMA((3,))],
        local_cost,
    )
    next_base = call(
        next_base_kernel,
        [KEPT, VMEM, VMEM, KEPT, VMEM],
        [
            pltpu.VMEM(whole, F32),
            pltpu.VMEM((2, rhs, 128), F32),
            pltpu.VMEM(whole, F32),
            pltpu.VMEM((17, rhs, 128), F32),
        ],
        [],
        local_cost,
    )
    owner = call(
        owner_kernel,
        [HBM, HBM, HBM, KEPT, KEPT, KEPT, KEPT],
        [pltpu.VMEM((slots, 40, 128), BF16)],
        [
            pltpu.SMEM(far_rank.shape, jnp.int32),
            pltpu.SMEM(block_pos.shape, jnp.int32),
            pltpu.VMEM(message, BF16),
            pltpu.VMEM(message, F32),
            pltpu.SemaphoreType.DMA((3,)),
        ],
    )
    leaf = call(
        leaf_kernel,
        [HBM, VMEM, KEPT, VMEM],
        [
            pltpu.VMEM(whole, F32),
            pltpu.VMEM(whole, F32),
            pltpu.VMEM((3, rhs, 128), F32),
            pltpu.HBM(message, BF16),
        ],
        [
            pltpu.SMEM((slots,), jnp.int32),
            pltpu.VMEM(whole, BF16),
            pltpu.VMEM(message, BF16),
            pltpu.SemaphoreType.DMA((5,)),
        ],
    )
    final = call(
        final_kernel,
        [HBM, VMEM, KEPT, VMEM, KEPT, KEPT, KEPT, KEPT, KEPT],
        [jax.ShapeDtypeStruct(whole, F32), jax.ShapeDtypeStruct(whole, F32)],
        [pltpu.SMEM((slots,), jnp.int32), pltpu.VMEM(whole, F32), pltpu.SemaphoreType.DMA],
    )

    with jax.named_scope("send"):
        (outgoing,) = send(targets, right_sides)
    incoming = swap(outgoing)
    with jax.named_scope("base"):
        base_image, small, near, left, right = base(
            right_sides, diag_shift, self_blocks, near_blocks, far_left, far_right
        )
    with jax.named_scope("owner"):
        (sums,) = owner(far_rank, block_pos, incoming, near, left, right, small)
    back = swap(sums)
    with jax.named_scope("leaf"):
        residual, image, old, outgoing = leaf(targets, back, base_image, right_sides)
    incoming = swap(outgoing)
    with jax.named_scope("base"):
        base_image, small, part, steps = next_base(
            residual, diag_shift, self_blocks, old, right_sides
        )
    with jax.named_scope("owner"):
        (sums,) = owner(far_rank, block_pos, incoming, near, left, right, small)
    back = swap(sums)
    with jax.named_scope("final"):
        answer, residual = final(
            targets, back, base_image, right_sides, residual, image, old, part, steps
        )
    return (answer, residual)


def solution(mesh):
    split = P(AXES, None, None)
    placed = (
        split,
        P(AXES, None),
        split,
        split,
        split,
        split,
        P(AXES),
        split,
        P(None, AXES),
    )
    return jax.shard_map(
        shards, mesh=mesh, in_specs=placed, out_specs=(split, split), check_vma=False
    )
```

```python
import jax
import jax.numpy as jnp
from jax import lax
from jax.experimental import pallas as pl
from jax.experimental.pallas import tpu as pltpu
from jax.sharding import PartitionSpec as P

AXES = ("clus", "grp")
KEPT_NEAR = 8
HIGHEST = lax.Precision.HIGHEST
NT = (((1,), (1,)), ((), ()))
F32 = jnp.float32
BF16 = jnp.bfloat16

VMEM = pl.BlockSpec(memory_space=pltpu.VMEM)
HBM = pl.BlockSpec(memory_space=pltpu.HBM)
KEPT = pl.BlockSpec(memory_space=pltpu.VMEM)


def iota(shape, dim):
    return lax.broadcasted_iota(jnp.int32, shape, dim)


def spread(values):
    values = values + pltpu.roll(values, 64, 1)
    values = values + pltpu.roll(values, 32, 1)
    return values + pltpu.roll(values, 16, 1)


def block_mask():
    return iota((128, 128), 0) // 16 == iota((128, 128), 1) // 16


def fold(products):
    kept = jnp.where(block_mask(), products, 0.0)
    total = kept[0:16]
    for part in range(1, 8):
        total = total + kept[16 * part : 16 * part + 16]
    return spread(total)


def kron_rows(coefs):
    tiled = jnp.concatenate([coefs] * 8, axis=0)
    return jnp.where(block_mask(), tiled, 0.0).T


def combine(field, kron):
    return jnp.dot(kron, field, precision=HIGHEST, preferred_element_type=F32)


def gram(left, right):
    return fold(lax.dot_general(left, right, NT, precision=HIGHEST, preferred_element_type=F32))


def columns(matrix):
    return [jnp.broadcast_to(matrix[:, at : at + 1], (16, 128)) for at in range(16)]


def factor(matrix):
    row_at = iota((16, 128), 0)
    left = columns(matrix)
    steps = []
    for step in range(16):
        column = left[step]
        pivot = column[step : step + 1]
        scale = jnp.where(pivot > 0, 1.0 / pivot, jnp.nan)
        steps.append((column, scale))
        for later in range(step + 1, 16):
            scaled = left[later][step : step + 1] * scale
            left[later] = jnp.where(row_at == step, scaled, left[later] - column * scaled)
    return steps


def apply_factor(steps, target):
    row_at = iota((16, 128), 0)
    for step, (column, scale) in enumerate(steps):
        scaled = target[step : step + 1] * scale
        target = jnp.where(row_at == step, scaled, target - column * scaled)
    return target


def solve(matrix, target):
    return apply_factor(factor(matrix), target)


def product(left, right):
    total = left[0] * right[0:1]
    for at in range(1, 16):
        total = total + left[at] * right[at : at + 1]
    return total


def pack(first, second):
    group = iota((8, 128), 1) // 16
    tile = jnp.zeros((8, 128), F32)
    at = 0
    for matrix in (first, second):
        high = matrix.astype(BF16).astype(F32)
        low = matrix - high
        for piece in (high, low):
            for half in (piece[0:8], piece[8:16]):
                tile = jnp.where(group == at, half, tile)
                at += 1
    return tile.astype(BF16)


def unpack(tile):
    group = iota((8, 128), 1) // 16
    joined = tile + pltpu.roll(tile, 128 - 32, 1)
    halves = [spread(jnp.where(group == at, joined, 0.0)) for at in (0, 1, 4, 5)]
    return jnp.concatenate(halves[0:2], axis=0), jnp.concatenate(halves[2:4], axis=0)


def fill(leaf_ref, half_ref, stage_ref, message_ref, sems):
    part = stage_ref.shape[0] // 4
    copies = []
    for quarter in range(4):

        def some(at, carry, first=quarter * part):
            for inner in range(8):
                owner = first + at * 8 + inner
                stage_ref[owner] = half_ref[leaf_ref[owner]]
            return carry

        lax.fori_loop(0, part // 8, some, 0)
        here = pl.ds(quarter * part, part)
        copy = pltpu.make_async_copy(stage_ref.at[here], message_ref.at[here], sems.at[quarter])
        copy.start()
        copies.append(copy)
    return copies


def send_kernel(leaf_hbm, field_hbm, message_ref, leaf_ref, field_ref, half_ref, stage_ref, sems):
    leaf_copy = pltpu.make_async_copy(leaf_hbm, leaf_ref, sems.at[4])
    field_copy = pltpu.make_async_copy(field_hbm, field_ref, sems.at[5])
    leaf_copy.start()
    field_copy.start()
    field_copy.wait()
    half_ref[...] = field_ref[...].astype(BF16)
    leaf_copy.wait()
    for copy in fill(leaf_ref, half_ref, stage_ref, message_ref, sems):
        copy.wait()


def local_product(field_ref, shift_ref, self_ref, base_ref, small_ref):
    for leaf in range(field_ref.shape[0]):
        field = field_ref[leaf]
        half = field.astype(BF16)
        block = self_ref[leaf]
        total = shift_ref[leaf : leaf + 1, :] * field
        total = total + lax.dot_general(half, block, NT, preferred_element_type=F32)
        base_ref[leaf] = total + jnp.dot(half, block, preferred_element_type=F32)
    fields = field_ref[...].reshape(128, 256)
    small_ref[0] = gram(fields, base_ref[...].reshape(128, 256))
    small_ref[1] = gram(fields, fields)


def base_kernel(
    field_ref, shift_ref, self_hbm, near_hbm, base_ref, small_ref, near_ref, self_ref, sems
):
    self_copy = pltpu.make_async_copy(self_hbm, self_ref, sems.at[0])
    near_copy = pltpu.make_async_copy(
        near_hbm.at[pl.ds(0, near_ref.shape[0])], near_ref, sems.at[1]
    )
    self_copy.start()
    near_copy.start()
    self_copy.wait()
    local_product(field_ref, shift_ref, self_ref, base_ref, small_ref)
    near_copy.wait()


def next_base_kernel(
    field_ref, shift_ref, self_hbm, old_ref, first_ref,
    base_ref, small_ref, part_ref, steps_ref, self_ref, sem,
):
    self_copy = pltpu.make_async_copy(self_hbm, self_ref, sem)
    self_copy.start()
    self_copy.wait()
    local_product(field_ref, shift_ref, self_ref, base_ref, small_ref)
    part = combine(first_ref[...].reshape(128, 256), kron_rows(old_ref[2]))
    part_ref[...] = part.reshape(part_ref.shape)
    for step, (column, scale) in enumerate(factor(old_ref[1])):
        steps_ref[step] = column
        steps_ref[16, step : step + 1] = scale


def owner_kernel(
    rank_hbm, at_hbm, x_ref, kept_ref, near_hbm, left_hbm, right_hbm, small_ref,
    out_ref, rank_ref, at_ref, near_ref, left_ref, right_ref, acc_ref, sems,
):
    kept = kept_ref.shape[0]
    streamed = near_ref.shape[0]
    near = kept + streamed
    slots = x_ref.shape[0]
    far = left_ref.shape[0]
    copies = [
        pltpu.make_async_copy(at_hbm, at_ref, sems.at[0]),
        pltpu.make_async_copy(near_hbm.at[pl.ds(kept, streamed)], near_ref, sems.at[1]),
        pltpu.make_async_copy(rank_hbm, rank_ref, sems.at[2]),
        pltpu.make_async_copy(left_hbm, left_ref, sems.at[3]),
        pltpu.make_async_copy(right_hbm, right_ref, sems.at[4]),
    ]
    for copy in copies:
        copy.start()

    def clear(at, carry):
        acc_ref[pl.ds(at * 8, 8)] = jnp.zeros((8, 16, 256), F32)
        return carry

    lax.fori_loop(0, slots // 8, clear, 0)
    copies[0].wait()

    def near_part(block_ref, shift):
        def some(at, carry):
            sums = []
            for part in range(8):
                which = at * 8 + part
                row, col = at_ref[0, shift + which], at_ref[1, shift + which]
                block = block_ref[which]
                sums.append(
                    (row, lax.dot_general(x_ref[col], block, NT, preferred_element_type=F32))
                )
                sums.append((col, jnp.dot(x_ref[row], block, preferred_element_type=F32)))
            for slot, value in sums:
                acc_ref[slot] += value
            return carry

        lax.fori_loop(0, block_ref.shape[0] // 8, some, 0)

    near_part(kept_ref, 0)
    copies[1].wait()
    near_part(near_ref, kept)
    for copy in copies[2:]:
        copy.wait()

    lane = iota((16, 256), 1)

    def far_project(first):
        left = left_ref[pl.ds(first, 8)].reshape(256, 256)
        right = right_ref[pl.ds(first, 8)].reshape(256, 256)
        rows = [at_ref[0, near + first + part] for part in range(8)]
        cols = [at_ref[1, near + first + part] for part in range(8)]
        x_row = jnp.concatenate([x_ref[slot] for slot in rows], axis=0)
        x_col = jnp.concatenate([x_ref[slot] for slot in cols], axis=0)
        kept = jnp.concatenate(
            [
                (lane >= 32 * part) & (lane < 32 * part + rank_ref[first + part])
                for part in range(8)
            ],
            axis=0,
        )
        right_proj = lax.dot_general(x_col, right, NT, preferred_element_type=F32)
        left_proj = lax.dot_general(x_row, left, NT, preferred_element_type=F32)
        right_proj = jnp.where(kept, right_proj, 0.0).astype(BF16)
        left_proj = jnp.where(kept, left_proj, 0.0).astype(BF16)
        return rows, cols, left, right, right_proj, left_proj

    def far_some(at, carry):
        sums = []
        for rows, cols, left, right, right_proj, left_proj in [
            far_project(at * 32 + 8 * group) for group in range(4)
        ]:
            to_row = jnp.dot(right_proj, left, preferred_element_type=F32)
            to_col = jnp.dot(left_proj, right, preferred_element_type=F32)
            for part in range(8):
                sums.append((rows[part], to_row[16 * part : 16 * part + 16]))
                sums.append((cols[part], to_col[16 * part : 16 * part + 16]))
        for slot, value in sums:
            acc_ref[slot] += value
        return carry

    lax.fori_loop(0, far // 32, far_some, 0)

    products = jnp.zeros((128, 128), F32)
    for at in range(slots // 8):
        here = slice(at * 8, at * 8 + 8)
        sums = acc_ref[here].astype(BF16)
        out_ref[here, 0:16, :] = sums[:, :, 0:128]
        out_ref[here, 16:32, :] = sums[:, :, 128:256]
        products = products + lax.dot_general(
            x_ref[here].reshape(128, 256),
            sums.reshape(128, 256),
            NT,
            preferred_element_type=F32,
        )
    tile = pack(fold(products) + small_ref[0], small_ref[1])

    def attach(at, carry):
        out_ref[pl.ds(at * 8, 8), 32:40, :] = jnp.broadcast_to(tile[None], (8, 8, 128))
        return carry

    lax.fori_loop(0, slots // 8, attach, 0)


def add_returned(leaf_ref, sums_ref, acc_ref):
    def some(at, tiles):
        for part in range(8):
            owner = at * 8 + part
            leaf = leaf_ref[owner]
            acc_ref[leaf, :, 0:128] += sums_ref[owner, 0:16, :].astype(F32)
            acc_ref[leaf, :, 128:256] += sums_ref[owner, 16:32, :].astype(F32)
            tiles = tiles + sums_ref[owner, 32:40, :].astype(F32)
        return tiles

    return lax.fori_loop(0, sums_ref.shape[0] // 8, some, jnp.zeros((8, 128), F32))


def leaf_kernel(
    leaf_hbm, sums_ref, base_ref, field_ref,
    residual_ref, image_ref, small_ref, message_ref,
    leaf_ref, half_ref, stage_ref, sems,
):
    leaf_copy = pltpu.make_async_copy(leaf_hbm, leaf_ref, sems.at[4])
    leaf_copy.start()
    image_ref[...] = base_ref[...]
    leaf_copy.wait()
    curve, norm = unpack(add_returned(leaf_ref, sums_ref, image_ref))
    step = solve(curve, norm)
    image = image_ref[...].reshape(128, 256)
    residual = field_ref[...].reshape(128, 256) - combine(image, kron_rows(step))
    half_ref[...] = residual.reshape(residual_ref.shape).astype(BF16)
    copies = fill(leaf_ref, half_ref, stage_ref, message_ref, sems)
    residual_ref[...] = residual.reshape(residual_ref.shape)
    small_ref[0] = curve
    small_ref[1] = norm
    small_ref[2] = step
    for copy in copies:
        copy.wait()


def final_kernel(
    leaf_hbm, sums_ref, base_ref, field_ref, residual_ref, image_ref, small_ref, part_ref, steps_ref,
    solution_ref, out_ref, leaf_ref, acc_ref, sem,
):
    leaf_copy = pltpu.make_async_copy(leaf_hbm, leaf_ref, sem)
    leaf_copy.start()
    acc_ref[...] = base_ref[...]
    leaf_copy.wait()
    curve, next_norm = unpack(add_returned(leaf_ref, sums_ref, acc_ref))
    steps = [(steps_ref[step], steps_ref[16, step : step + 1]) for step in range(16)]
    coef = apply_factor(steps, next_norm)
    moved = product(columns(small_ref[0]), coef)
    moved = product(columns(coef.T[0:16]), moved)
    step = solve(curve - moved, next_norm)
    kron_coef = kron_rows(coef)
    residual = residual_ref[...].reshape(128, 256)
    direction = residual + combine(field_ref[...].reshape(128, 256), kron_coef)
    image = acc_ref[...].reshape(128, 256) + combine(
        image_ref[...].reshape(128, 256), kron_coef
    )
    kron_step = kron_rows(step)
    answer = part_ref[...].reshape(128, 256) + combine(direction, kron_step)
    solution_ref[...] = answer.reshape(solution_ref.shape)
    out_ref[...] = (residual - combine(image, kron_step)).reshape(out_ref.shape)


def call(kernel, ins, outs, scratch, cost=None):
    spaces = [HBM if getattr(out, "memory_space", None) == pltpu.HBM else VMEM for out in outs]
    run = pl.pallas_call(
        kernel,
        out_shape=list(outs),
        in_specs=list(ins),
        out_specs=spaces,
        scratch_shapes=list(scratch),
        compiler_params=pltpu.CompilerParams(vmem_limit_bytes=24 * 1024 * 1024),
        cost_estimate=cost,
    )

    def placed(*values):
        return run(
            *(
                pltpu.with_memory_space_constraint(value, spec.memory_space)
                if spec is HBM or spec is KEPT
                else value
                for value, spec in zip(values, ins)
            )
        )

    return placed


def swap(values):
    return lax.all_to_all(values, AXES, split_axis=0, concat_axis=0, tiled=True)


def shards(
    right_sides,
    diag_shift,
    self_blocks,
    near_blocks,
    far_left,
    far_right,
    far_rank,
    send_leaf,
    block_pos,
):
    leaves, rhs, size = right_sides.shape
    slots = send_leaf.shape[1]
    targets = send_leaf.reshape(slots)
    whole = (leaves, rhs, size)
    message = (slots, rhs, size)
    local_cost = pl.CostEstimate(
        flops=4 * leaves * rhs * size * size, bytes_accessed=2 * leaves * size * size, transcendentals=0
    )
    send = call(
        send_kernel,
        [HBM, HBM],
        [pltpu.HBM(message, BF16)],
        [
            pltpu.SMEM((slots,), jnp.int32),
            pltpu.VMEM(whole, F32),
            pltpu.VMEM(whole, BF16),
            pltpu.VMEM(message, BF16),
            pltpu.SemaphoreType.DMA((6,)),
        ],
    )
    base = call(
        base_kernel,
        [VMEM, VMEM, HBM, HBM],
        [
            pltpu.VMEM(whole, F32),
            pltpu.VMEM((2, rhs, 128), F32),
            pltpu.VMEM((KEPT_NEAR, size, size), BF16),
        ],
        [pltpu.VMEM(self_blocks.shape, BF16), pltpu.SemaphoreType.DMA((2,))],
        local_cost,
    )
    next_base = call(
        next_base_kernel,
        [KEPT, VMEM, HBM, KEPT, VMEM],
        [
            pltpu.VMEM(whole, F32),
            pltpu.VMEM((2, rhs, 128), F32),
            pltpu.VMEM(whole, F32),
            pltpu.VMEM((17, rhs, 128), F32),
        ],
        [pltpu.VMEM(self_blocks.shape, BF16), pltpu.SemaphoreType.DMA],
        local_cost,
    )
    owner = call(
        owner_kernel,
        [HBM, HBM, VMEM, KEPT, HBM, HBM, HBM, KEPT],
        [pltpu.VMEM((slots, 40, 128), BF16)],
        [
            pltpu.SMEM(far_rank.shape, jnp.int32),
            pltpu.SMEM(block_pos.shape, jnp.int32),
            pltpu.VMEM((near_blocks.shape[0] - KEPT_NEAR, size, size), BF16),
            pltpu.VMEM(far_left.shape, BF16),
            pltpu.VMEM(far_right.shape, BF16),
            pltpu.VMEM(message, F32),
            pltpu.SemaphoreType.DMA((5,)),
        ],
    )
    leaf = call(
        leaf_kernel,
        [HBM, VMEM, KEPT, VMEM],
        [
            pltpu.VMEM(whole, F32),
            pltpu.VMEM(whole, F32),
            pltpu.VMEM((3, rhs, 128), F32),
            pltpu.HBM(message, BF16),
        ],
        [
            pltpu.SMEM((slots,), jnp.int32),
            pltpu.VMEM(whole, BF16),
            pltpu.VMEM(message, BF16),
            pltpu.SemaphoreType.DMA((5,)),
        ],
    )
    final = call(
        final_kernel,
        [HBM, VMEM, KEPT, VMEM, KEPT, KEPT, KEPT, KEPT, KEPT],
        [jax.ShapeDtypeStruct(whole, F32), jax.ShapeDtypeStruct(whole, F32)],
        [pltpu.SMEM((slots,), jnp.int32), pltpu.VMEM(whole, F32), pltpu.SemaphoreType.DMA],
    )

    with jax.named_scope("send"):
        (outgoing,) = send(targets, right_sides)
    incoming = swap(outgoing)
    with jax.named_scope("base"):
        base_image, small, kept = base(
            right_sides, diag_shift, self_blocks, near_blocks
        )
    with jax.named_scope("owner"):
        (sums,) = owner(far_rank, block_pos, incoming, kept, near_blocks, far_left, far_right, small)
    back = swap(sums)
    with jax.named_scope("leaf"):
        residual, image, old, outgoing = leaf(targets, back, base_image, right_sides)
    incoming = swap(outgoing)
    with jax.named_scope("base"):
        base_image, small, part, steps = next_base(
            residual, diag_shift, self_blocks, old, right_sides
        )
    with jax.named_scope("owner"):
        (sums,) = owner(far_rank, block_pos, incoming, kept, near_blocks, far_left, far_right, small)
    back = swap(sums)
    with jax.named_scope("final"):
        answer, residual = final(
            targets, back, base_image, right_sides, residual, image, old, part, steps
        )
    return (answer, residual)


def solution(mesh):
    split = P(AXES, None, None)
    placed = (
        split,
        P(AXES, None),
        split,
        split,
        split,
        split,
        P(AXES),
        split,
        P(None, AXES),
    )
    return jax.shard_map(
        shards, mesh=mesh, in_specs=placed, out_specs=(split, split), check_vma=False
    )
```

```python
import jax
import jax.numpy as jnp
from jax import lax
from jax.experimental import pallas as pl
from jax.experimental.pallas import tpu as pltpu
from jax.sharding import PartitionSpec as P

AXES = ("clus", "grp")
KEPT_NEAR = 8
HIGHEST = lax.Precision.HIGHEST
NT = (((1,), (1,)), ((), ()))
F32 = jnp.float32
BF16 = jnp.bfloat16

VMEM = pl.BlockSpec(memory_space=pltpu.VMEM)
HBM = pl.BlockSpec(memory_space=pltpu.HBM)
KEPT = pl.BlockSpec(memory_space=pltpu.VMEM)
TABLE = pl.BlockSpec(memory_space=pltpu.SMEM)


def iota(shape, dim):
    return lax.broadcasted_iota(jnp.int32, shape, dim)


def spread(values):
    values = values + pltpu.roll(values, 64, 1)
    values = values + pltpu.roll(values, 32, 1)
    return values + pltpu.roll(values, 16, 1)


def block_mask():
    return iota((128, 128), 0) // 16 == iota((128, 128), 1) // 16


def fold(products):
    kept = jnp.where(block_mask(), products, 0.0)
    total = kept[0:16]
    for part in range(1, 8):
        total = total + kept[16 * part : 16 * part + 16]
    return spread(total)


def kron_rows(coefs):
    tiled = jnp.concatenate([coefs] * 8, axis=0)
    return jnp.where(block_mask(), tiled, 0.0).T


def combine(field, kron):
    return jnp.dot(kron, field, precision=HIGHEST, preferred_element_type=F32)


def gram(left, right):
    return fold(lax.dot_general(left, right, NT, precision=HIGHEST, preferred_element_type=F32))


def columns(matrix):
    return [jnp.broadcast_to(matrix[:, at : at + 1], (16, 128)) for at in range(16)]


def factor(parts):
    row_at = iota((16, 128), 0)
    left = list(parts)
    steps = []
    for step in range(16):
        column = left[step]
        pivot = column[step : step + 1]
        scale = jnp.where(pivot > 0, 1.0 / pivot, jnp.nan)
        steps.append((column, scale))
        for later in range(step + 1, 16):
            scaled = left[later][step : step + 1] * scale
            left[later] = jnp.where(row_at == step, scaled, left[later] - column * scaled)
    return steps


def apply_factor(steps, target):
    row_at = iota((16, 128), 0)
    for step, (column, scale) in enumerate(steps):
        scaled = target[step : step + 1] * scale
        target = jnp.where(row_at == step, scaled, target - column * scaled)
    return target


def solve(parts, target):
    return apply_factor(factor(parts), target)


def product(left, right):
    total = left[0] * right[0:1]
    for at in range(1, 16):
        total = total + left[at] * right[at : at + 1]
    return total


def pack(first, second):
    group = iota((8, 128), 1) // 16
    tile = jnp.zeros((8, 128), F32)
    at = 0
    for matrix in (first, second):
        high = matrix.astype(BF16).astype(F32)
        low = matrix - high
        for piece in (high, low):
            for half in (piece[0:8], piece[8:16]):
                tile = jnp.where(group == at, half, tile)
                at += 1
    return tile.astype(BF16)


def unpack(tile):
    group = iota((8, 128), 1) // 16
    joined = tile + pltpu.roll(tile, 128 - 32, 1)
    first = [
        jnp.concatenate(
            [
                jnp.broadcast_to(joined[:, at : at + 1], (8, 128)),
                jnp.broadcast_to(joined[:, 16 + at : 17 + at], (8, 128)),
            ],
            axis=0,
        )
        for at in range(16)
    ]
    halves = [spread(jnp.where(group == at, joined, 0.0)) for at in (4, 5)]
    return first, jnp.concatenate(halves, axis=0)


def from_columns(parts):
    group = iota((16, 128), 1) % 16
    matrix = parts[0]
    for at in range(1, 16):
        matrix = jnp.where(group == at, parts[at], matrix)
    return matrix


def fill(leaf_ref, half_ref, stage_ref, message_ref, sems):
    part = stage_ref.shape[0] // 4
    copies = []
    for quarter in range(4):

        def some(at, carry, first=quarter * part):
            for inner in range(8):
                owner = first + at * 8 + inner
                stage_ref[owner] = half_ref[leaf_ref[owner]]
            return carry

        lax.fori_loop(0, part // 8, some, 0)
        here = pl.ds(quarter * part, part)
        copy = pltpu.make_async_copy(stage_ref.at[here], message_ref.at[here], sems.at[quarter])
        copy.start()
        copies.append(copy)
    return copies


def send_kernel(leaf_hbm, field_hbm, message_ref, leaf_ref, field_ref, half_ref, stage_ref, sems):
    leaf_copy = pltpu.make_async_copy(leaf_hbm, leaf_ref, sems.at[4])
    field_copy = pltpu.make_async_copy(field_hbm, field_ref, sems.at[5])
    leaf_copy.start()
    field_copy.start()
    field_copy.wait()
    half_ref[...] = field_ref[...].astype(BF16)
    leaf_copy.wait()
    for copy in fill(leaf_ref, half_ref, stage_ref, message_ref, sems):
        copy.wait()


def local_product(field_ref, shift_ref, self_ref, base_ref, small_ref):
    for leaf in range(field_ref.shape[0]):
        field = field_ref[leaf]
        half = field.astype(BF16)
        block = self_ref[leaf]
        total = shift_ref[leaf : leaf + 1, :] * field
        total = total + lax.dot_general(half, block, NT, preferred_element_type=F32)
        base_ref[leaf] = total + jnp.dot(half, block, preferred_element_type=F32)
    fields = field_ref[...].reshape(128, 256)
    small_ref[0] = gram(fields, base_ref[...].reshape(128, 256))
    small_ref[1] = gram(fields, fields)


def base_kernel(
    field_ref, shift_ref, self_hbm, near_hbm, leaf_hbm, rank_hbm, at_hbm,
    base_ref, small_ref, near_ref, leaf_ref, rank_ref, at_ref, self_ref, sems,
):
    tables = [
        pltpu.make_async_copy(leaf_hbm, leaf_ref, sems.at[2]),
        pltpu.make_async_copy(rank_hbm, rank_ref, sems.at[3]),
        pltpu.make_async_copy(at_hbm, at_ref, sems.at[4]),
    ]
    for table in tables:
        table.start()
    self_copy = pltpu.make_async_copy(self_hbm, self_ref, sems.at[0])
    near_copy = pltpu.make_async_copy(
        near_hbm.at[pl.ds(0, near_ref.shape[0])], near_ref, sems.at[1]
    )
    self_copy.start()
    near_copy.start()
    self_copy.wait()
    local_product(field_ref, shift_ref, self_ref, base_ref, small_ref)
    near_copy.wait()
    for table in tables:
        table.wait()


def next_base_kernel(
    field_ref, shift_ref, self_hbm, old_ref, first_ref,
    base_ref, small_ref, part_ref, steps_ref, self_ref, sem,
):
    self_copy = pltpu.make_async_copy(self_hbm, self_ref, sem)
    self_copy.start()
    self_copy.wait()
    local_product(field_ref, shift_ref, self_ref, base_ref, small_ref)
    part = combine(first_ref[...].reshape(128, 256), kron_rows(old_ref[2]))
    part_ref[...] = part.reshape(part_ref.shape)
    for step, (column, scale) in enumerate(factor(columns(old_ref[1]))):
        steps_ref[step] = column
        steps_ref[16, step : step + 1] = scale


def owner_kernel(
    rank_ref, at_ref, x_ref, kept_ref, near_hbm, left_hbm, right_hbm, small_ref,
    out_ref, near_ref, left_ref, right_ref, acc_ref, sems,
):
    kept = kept_ref.shape[0]
    streamed = near_ref.shape[0]
    near = kept + streamed
    slots = x_ref.shape[0]
    far = left_ref.shape[0]
    copies = [
        pltpu.make_async_copy(near_hbm.at[pl.ds(kept, streamed)], near_ref, sems.at[0]),
        pltpu.make_async_copy(left_hbm, left_ref, sems.at[1]),
        pltpu.make_async_copy(right_hbm, right_ref, sems.at[2]),
    ]
    for copy in copies:
        copy.start()

    def clear(at, carry):
        acc_ref[pl.ds(at * 8, 8)] = jnp.zeros((8, 16, 256), F32)
        return carry

    lax.fori_loop(0, slots // 8, clear, 0)

    def near_part(block_ref, shift):
        sums = []
        for which in range(block_ref.shape[0]):
            row, col = at_ref[0, shift + which], at_ref[1, shift + which]
            block = block_ref[which]
            sums.append(
                (row, lax.dot_general(x_ref[col], block, NT, preferred_element_type=F32))
            )
            sums.append((col, jnp.dot(x_ref[row], block, preferred_element_type=F32)))
        for slot, value in sums:
            acc_ref[slot] += value

    near_part(kept_ref, 0)
    copies[0].wait()
    near_part(near_ref, kept)
    for copy in copies[1:]:
        copy.wait()

    lane = iota((16, 256), 1)

    def far_project(first):
        left = left_ref[pl.ds(first, 8)].reshape(256, 256)
        right = right_ref[pl.ds(first, 8)].reshape(256, 256)
        rows = [at_ref[0, near + first + part] for part in range(8)]
        cols = [at_ref[1, near + first + part] for part in range(8)]
        x_row = jnp.concatenate([x_ref[slot] for slot in rows], axis=0)
        x_col = jnp.concatenate([x_ref[slot] for slot in cols], axis=0)
        kept = jnp.concatenate(
            [
                (lane >= 32 * part) & (lane < 32 * part + rank_ref[first + part])
                for part in range(8)
            ],
            axis=0,
        )
        right_proj = lax.dot_general(x_col, right, NT, preferred_element_type=F32)
        left_proj = lax.dot_general(x_row, left, NT, preferred_element_type=F32)
        right_proj = jnp.where(kept, right_proj, 0.0).astype(BF16)
        left_proj = jnp.where(kept, left_proj, 0.0).astype(BF16)
        return rows, cols, left, right, right_proj, left_proj

    def far_some(at, carry):
        sums = []
        for rows, cols, left, right, right_proj, left_proj in [
            far_project(at * 48 + 8 * group) for group in range(6)
        ]:
            to_row = jnp.dot(right_proj, left, preferred_element_type=F32)
            to_col = jnp.dot(left_proj, right, preferred_element_type=F32)
            for part in range(8):
                sums.append((rows[part], to_row[16 * part : 16 * part + 16]))
                sums.append((cols[part], to_col[16 * part : 16 * part + 16]))
        for slot, value in sums:
            acc_ref[slot] += value
        return carry

    lax.fori_loop(0, far // 48, far_some, 0)

    products = jnp.zeros((128, 128), F32)
    for at in range(slots // 8):
        here = slice(at * 8, at * 8 + 8)
        sums = acc_ref[here].astype(BF16)
        out_ref[here, 0:16, :] = sums[:, :, 0:128]
        out_ref[here, 16:32, :] = sums[:, :, 128:256]
        products = products + lax.dot_general(
            x_ref[here].reshape(128, 256),
            sums.reshape(128, 256),
            NT,
            preferred_element_type=F32,
        )
    tile = pack(fold(products) + small_ref[0], small_ref[1])

    def attach(at, carry):
        out_ref[pl.ds(at * 8, 8), 32:40, :] = jnp.broadcast_to(tile[None], (8, 8, 128))
        return carry

    lax.fori_loop(0, slots // 8, attach, 0)


def add_returned(leaf_ref, sums_ref, acc_ref):
    def some(at, tiles):
        for part in range(8):
            owner = at * 8 + part
            leaf = leaf_ref[owner]
            acc_ref[leaf, :, 0:128] += sums_ref[owner, 0:16, :].astype(F32)
            acc_ref[leaf, :, 128:256] += sums_ref[owner, 16:32, :].astype(F32)
            tiles = tiles + sums_ref[owner, 32:40, :].astype(F32)
        return tiles

    return lax.fori_loop(0, sums_ref.shape[0] // 8, some, jnp.zeros((8, 128), F32))


def leaf_kernel(
    leaf_ref, sums_ref, base_ref, field_ref,
    residual_ref, image_ref, small_ref, message_ref,
    half_ref, stage_ref, sems,
):
    image_ref[...] = base_ref[...]
    curve, norm = unpack(add_returned(leaf_ref, sums_ref, image_ref))
    step = solve(curve, norm)
    image = image_ref[...].reshape(128, 256)
    residual = field_ref[...].reshape(128, 256) - combine(image, kron_rows(step))
    half_ref[...] = residual.reshape(residual_ref.shape).astype(BF16)
    copies = fill(leaf_ref, half_ref, stage_ref, message_ref, sems)
    residual_ref[...] = residual.reshape(residual_ref.shape)
    small_ref[0] = from_columns(curve)
    small_ref[1] = norm
    small_ref[2] = step
    for copy in copies:
        copy.wait()


def final_kernel(
    leaf_ref, sums_ref, base_ref, field_ref, residual_ref, image_ref, small_ref, part_ref, steps_ref,
    solution_ref, out_ref, acc_ref,
):
    acc_ref[...] = base_ref[...]
    curve, next_norm = unpack(add_returned(leaf_ref, sums_ref, acc_ref))
    steps = [(steps_ref[step], steps_ref[16, step : step + 1]) for step in range(16)]
    coef = apply_factor(steps, next_norm)
    moved = product(columns(small_ref[0]), coef)
    moved = product(columns(coef.T[0:16]), moved)
    moved = columns(moved)
    step = solve([curve[at] - moved[at] for at in range(16)], next_norm)
    kron_coef = kron_rows(coef)
    residual = residual_ref[...].reshape(128, 256)
    direction = residual + combine(field_ref[...].reshape(128, 256), kron_coef)
    image = acc_ref[...].reshape(128, 256) + combine(
        image_ref[...].reshape(128, 256), kron_coef
    )
    kron_step = kron_rows(step)
    answer = part_ref[...].reshape(128, 256) + combine(direction, kron_step)
    solution_ref[...] = answer.reshape(solution_ref.shape)
    out_ref[...] = (residual - combine(image, kron_step)).reshape(out_ref.shape)


def call(kernel, ins, outs, scratch, cost=None):
    kinds = {pltpu.HBM: HBM, pltpu.SMEM: TABLE}
    spaces = [kinds.get(getattr(out, "memory_space", None), VMEM) for out in outs]
    run = pl.pallas_call(
        kernel,
        out_shape=list(outs),
        in_specs=list(ins),
        out_specs=spaces,
        scratch_shapes=list(scratch),
        compiler_params=pltpu.CompilerParams(vmem_limit_bytes=24 * 1024 * 1024),
        cost_estimate=cost,
    )

    def placed(*values):
        return run(
            *(
                pltpu.with_memory_space_constraint(value, spec.memory_space)
                if spec is not VMEM
                else value
                for value, spec in zip(values, ins)
            )
        )

    return placed


def swap(values):
    return lax.all_to_all(values, AXES, split_axis=0, concat_axis=0, tiled=True)


def shards(
    right_sides,
    diag_shift,
    self_blocks,
    near_blocks,
    far_left,
    far_right,
    far_rank,
    send_leaf,
    block_pos,
):
    leaves, rhs, size = right_sides.shape
    slots = send_leaf.shape[1]
    targets = send_leaf.reshape(slots)
    whole = (leaves, rhs, size)
    message = (slots, rhs, size)
    local_cost = pl.CostEstimate(
        flops=4 * leaves * rhs * size * size, bytes_accessed=2 * leaves * size * size, transcendentals=0
    )
    send = call(
        send_kernel,
        [HBM, HBM],
        [pltpu.HBM(message, BF16)],
        [
            pltpu.SMEM((slots,), jnp.int32),
            pltpu.VMEM(whole, F32),
            pltpu.VMEM(whole, BF16),
            pltpu.VMEM(message, BF16),
            pltpu.SemaphoreType.DMA((6,)),
        ],
    )
    base = call(
        base_kernel,
        [VMEM, VMEM, HBM, HBM, HBM, HBM, HBM],
        [
            pltpu.VMEM(whole, F32),
            pltpu.VMEM((2, rhs, 128), F32),
            pltpu.VMEM((KEPT_NEAR, size, size), BF16),
            pltpu.SMEM((slots,), jnp.int32),
            pltpu.SMEM(far_rank.shape, jnp.int32),
            pltpu.SMEM(block_pos.shape, jnp.int32),
        ],
        [pltpu.VMEM(self_blocks.shape, BF16), pltpu.SemaphoreType.DMA((5,))],
        local_cost,
    )
    next_base = call(
        next_base_kernel,
        [KEPT, VMEM, HBM, KEPT, VMEM],
        [
            pltpu.VMEM(whole, F32),
            pltpu.VMEM((2, rhs, 128), F32),
            pltpu.VMEM(whole, F32),
            pltpu.VMEM((17, rhs, 128), F32),
        ],
        [pltpu.VMEM(self_blocks.shape, BF16), pltpu.SemaphoreType.DMA],
        local_cost,
    )
    owner = call(
        owner_kernel,
        [TABLE, TABLE, VMEM, KEPT, HBM, HBM, HBM, KEPT],
        [pltpu.VMEM((slots, 40, 128), BF16)],
        [
            pltpu.VMEM((near_blocks.shape[0] - KEPT_NEAR, size, size), BF16),
            pltpu.VMEM(far_left.shape, BF16),
            pltpu.VMEM(far_right.shape, BF16),
            pltpu.VMEM(message, F32),
            pltpu.SemaphoreType.DMA((3,)),
        ],
    )
    leaf = call(
        leaf_kernel,
        [TABLE, VMEM, KEPT, VMEM],
        [
            pltpu.VMEM(whole, F32),
            pltpu.VMEM(whole, F32),
            pltpu.VMEM((3, rhs, 128), F32),
            pltpu.HBM(message, BF16),
        ],
        [
            pltpu.VMEM(whole, BF16),
            pltpu.VMEM(message, BF16),
            pltpu.SemaphoreType.DMA((4,)),
        ],
    )
    final = call(
        final_kernel,
        [TABLE, VMEM, KEPT, VMEM, KEPT, KEPT, KEPT, KEPT, KEPT],
        [jax.ShapeDtypeStruct(whole, F32), jax.ShapeDtypeStruct(whole, F32)],
        [pltpu.VMEM(whole, F32)],
    )

    with jax.named_scope("send"):
        (outgoing,) = send(targets, right_sides)
    incoming = swap(outgoing)
    with jax.named_scope("base"):
        base_image, small, kept, leaf_table, rank_table, at_table = base(
            right_sides, diag_shift, self_blocks, near_blocks, targets, far_rank, block_pos
        )
    with jax.named_scope("owner"):
        (sums,) = owner(
            rank_table, at_table, incoming, kept, near_blocks, far_left, far_right, small
        )
    back = swap(sums)
    with jax.named_scope("leaf"):
        residual, image, old, outgoing = leaf(leaf_table, back, base_image, right_sides)
    incoming = swap(outgoing)
    with jax.named_scope("base"):
        base_image, small, part, steps = next_base(
            residual, diag_shift, self_blocks, old, right_sides
        )
    with jax.named_scope("owner"):
        (sums,) = owner(
            rank_table, at_table, incoming, kept, near_blocks, far_left, far_right, small
        )
    back = swap(sums)
    with jax.named_scope("final"):
        answer, residual = final(
            leaf_table, back, base_image, right_sides, residual, image, old, part, steps
        )
    return (answer, residual)


def solution(mesh):
    split = P(AXES, None, None)
    placed = (
        split,
        P(AXES, None),
        split,
        split,
        split,
        split,
        P(AXES),
        split,
        P(None, AXES),
    )
    return jax.shard_map(
        shards, mesh=mesh, in_specs=placed, out_specs=(split, split), check_vma=False
    )
```

```python
import jax
import jax.numpy as jnp
from jax import lax
from jax.experimental import pallas as pl
from jax.experimental.pallas import tpu as pltpu
from jax.sharding import PartitionSpec as P

AXES = ("clus", "grp")
KEPT_NEAR = 8
QUARTERS = 4
HIGHEST = lax.Precision.HIGHEST
NT = (((1,), (1,)), ((), ()))
F32 = jnp.float32
BF16 = jnp.bfloat16

VMEM = pl.BlockSpec(memory_space=pltpu.VMEM)
HBM = pl.BlockSpec(memory_space=pltpu.HBM)
KEPT = pl.BlockSpec(memory_space=pltpu.VMEM)
TABLE = pl.BlockSpec(memory_space=pltpu.SMEM)


def iota(shape, dim):
    return lax.broadcasted_iota(jnp.int32, shape, dim)


def spread(values):
    values = values + pltpu.roll(values, 64, 1)
    values = values + pltpu.roll(values, 32, 1)
    return values + pltpu.roll(values, 16, 1)


def block_mask():
    return iota((128, 128), 0) // 16 == iota((128, 128), 1) // 16


def fold(products):
    kept = jnp.where(block_mask(), products, 0.0)
    total = kept[0:16]
    for part in range(1, 8):
        total = total + kept[16 * part : 16 * part + 16]
    return spread(total)


def kron_rows(coefs):
    tiled = jnp.concatenate([coefs] * 8, axis=0)
    return jnp.where(block_mask(), tiled, 0.0).T


def combine(field, kron):
    return jnp.dot(kron, field, precision=HIGHEST, preferred_element_type=F32)


def gram(left, right):
    return fold(lax.dot_general(left, right, NT, precision=HIGHEST, preferred_element_type=F32))


def columns(matrix):
    return [jnp.broadcast_to(matrix[:, at : at + 1], (16, 128)) for at in range(16)]


def factor(parts):
    row_at = iota((16, 128), 0)
    left = list(parts)
    steps = []
    for step in range(16):
        column = left[step]
        pivot = column[step : step + 1]
        scale = jnp.where(pivot > 0, 1.0 / pivot, jnp.nan)
        steps.append((column, scale))
        for later in range(step + 1, 16):
            scaled = left[later][step : step + 1] * scale
            left[later] = jnp.where(row_at == step, scaled, left[later] - column * scaled)
    return steps


def apply_factor(steps, target):
    row_at = iota((16, 128), 0)
    for step, (column, scale) in enumerate(steps):
        scaled = target[step : step + 1] * scale
        target = jnp.where(row_at == step, scaled, target - column * scaled)
    return target


def solve(parts, target):
    return apply_factor(factor(parts), target)


def product(left, right):
    total = left[0] * right[0:1]
    for at in range(1, 16):
        total = total + left[at] * right[at : at + 1]
    return total


def pack(first, second):
    group = iota((8, 128), 1) // 16
    tile = jnp.zeros((8, 128), F32)
    at = 0
    for matrix in (first, second):
        high = matrix.astype(BF16).astype(F32)
        low = matrix - high
        for piece in (high, low):
            for half in (piece[0:8], piece[8:16]):
                tile = jnp.where(group == at, half, tile)
                at += 1
    return tile.astype(BF16)


def unpack(tile):
    group = iota((8, 128), 1) // 16
    joined = tile + pltpu.roll(tile, 128 - 32, 1)
    first = [
        jnp.concatenate(
            [
                jnp.broadcast_to(joined[:, at : at + 1], (8, 128)),
                jnp.broadcast_to(joined[:, 16 + at : 17 + at], (8, 128)),
            ],
            axis=0,
        )
        for at in range(16)
    ]
    halves = [spread(jnp.where(group == at, joined, 0.0)) for at in (4, 5)]
    return first, jnp.concatenate(halves, axis=0)


def from_columns(parts):
    group = iota((16, 128), 1) % 16
    matrix = parts[0]
    for at in range(1, 16):
        matrix = jnp.where(group == at, parts[at], matrix)
    return matrix


def fill(leaf_ref, half_ref, stage_ref, message_ref, sems):
    part = stage_ref.shape[0] // 4
    copies = []
    for quarter in range(4):

        def some(at, carry, first=quarter * part):
            for inner in range(8):
                owner = first + at * 8 + inner
                stage_ref[owner] = half_ref[leaf_ref[owner]]
            return carry

        lax.fori_loop(0, part // 8, some, 0)
        here = pl.ds(quarter * part, part)
        copy = pltpu.make_async_copy(stage_ref.at[here], message_ref.at[here], sems.at[quarter])
        copy.start()
        copies.append(copy)
    return copies


def send_kernel(leaf_hbm, field_hbm, message_ref, leaf_ref, field_ref, half_ref, stage_ref, sems):
    leaf_copy = pltpu.make_async_copy(leaf_hbm, leaf_ref, sems.at[4])
    field_copy = pltpu.make_async_copy(field_hbm, field_ref, sems.at[5])
    leaf_copy.start()
    field_copy.start()
    field_copy.wait()
    half_ref[...] = field_ref[...].astype(BF16)
    leaf_copy.wait()
    for copy in fill(leaf_ref, half_ref, stage_ref, message_ref, sems):
        copy.wait()


def local_product(field_ref, shift_ref, self_ref, base_ref, small_ref):
    for leaf in range(field_ref.shape[0]):
        field = field_ref[leaf]
        half = field.astype(BF16)
        block = self_ref[leaf]
        total = shift_ref[leaf : leaf + 1, :] * field
        total = total + lax.dot_general(half, block, NT, preferred_element_type=F32)
        base_ref[leaf] = total + jnp.dot(half, block, preferred_element_type=F32)
    fields = field_ref[...].reshape(128, 256)
    small_ref[0] = gram(fields, base_ref[...].reshape(128, 256))
    small_ref[1] = gram(fields, fields)


def base_kernel(
    field_ref, shift_ref, self_hbm, near_hbm, leaf_hbm, rank_hbm, at_hbm,
    base_ref, small_ref, near_ref, leaf_ref, rank_ref, at_ref, self_ref, sems,
):
    tables = [
        pltpu.make_async_copy(leaf_hbm, leaf_ref, sems.at[2]),
        pltpu.make_async_copy(rank_hbm, rank_ref, sems.at[3]),
        pltpu.make_async_copy(at_hbm, at_ref, sems.at[4]),
    ]
    for table in tables:
        table.start()
    self_copy = pltpu.make_async_copy(self_hbm, self_ref, sems.at[0])
    near_copy = pltpu.make_async_copy(
        near_hbm.at[pl.ds(0, near_ref.shape[0])], near_ref, sems.at[1]
    )
    self_copy.start()
    near_copy.start()
    self_copy.wait()
    local_product(field_ref, shift_ref, self_ref, base_ref, small_ref)
    near_copy.wait()
    for table in tables:
        table.wait()


def next_base_kernel(
    field_ref, shift_ref, self_hbm, old_ref, first_ref,
    base_ref, small_ref, part_ref, steps_ref, self_ref, sem,
):
    self_copy = pltpu.make_async_copy(self_hbm, self_ref, sem)
    self_copy.start()
    self_copy.wait()
    local_product(field_ref, shift_ref, self_ref, base_ref, small_ref)
    part = combine(first_ref[...].reshape(128, 256), kron_rows(old_ref[2]))
    part_ref[...] = part.reshape(part_ref.shape)
    for step, (column, scale) in enumerate(factor(columns(old_ref[1]))):
        steps_ref[step] = column
        steps_ref[16, step : step + 1] = scale


def owner_kernel(
    rank_ref, at_ref, x_ref, kept_ref, near_hbm, left_hbm, right_hbm, small_ref,
    out_ref, near_ref, left_ref, right_ref, acc_ref, sems,
):
    kept = kept_ref.shape[0]
    streamed = near_ref.shape[0]
    near = kept + streamed
    slots = x_ref.shape[0]
    far = left_ref.shape[0]
    near_step = streamed // QUARTERS
    far_step = far // QUARTERS
    copies = []
    for quarter in range(QUARTERS):
        near_from = quarter * near_step
        far_here = pl.ds(quarter * far_step, far_step)
        copies.append(
            [
                pltpu.make_async_copy(
                    near_hbm.at[pl.ds(kept + near_from, near_step)],
                    near_ref.at[pl.ds(near_from, near_step)],
                    sems.at[quarter, 0],
                ),
                pltpu.make_async_copy(left_hbm.at[far_here], left_ref.at[far_here], sems.at[quarter, 1]),
                pltpu.make_async_copy(right_hbm.at[far_here], right_ref.at[far_here], sems.at[quarter, 2]),
            ]
        )
        for copy in copies[quarter]:
            copy.start()

    def clear(at, carry):
        acc_ref[pl.ds(at * 8, 8)] = jnp.zeros((8, 16, 256), F32)
        return carry

    lax.fori_loop(0, slots // 8, clear, 0)

    def near_sums(block_ref, first, count, shift):
        sums = []
        for which in range(first, first + count):
            row, col = at_ref[0, shift + which], at_ref[1, shift + which]
            block = block_ref[which]
            sums.append(
                (row, lax.dot_general(x_ref[col], block, NT, preferred_element_type=F32))
            )
            sums.append((col, jnp.dot(x_ref[row], block, preferred_element_type=F32)))
        return sums

    lane = iota((16, 256), 1)

    def far_project(first):
        left = left_ref[pl.ds(first, 8)].reshape(256, 256)
        right = right_ref[pl.ds(first, 8)].reshape(256, 256)
        rows = [at_ref[0, near + first + part] for part in range(8)]
        cols = [at_ref[1, near + first + part] for part in range(8)]
        x_row = jnp.concatenate([x_ref[slot] for slot in rows], axis=0)
        x_col = jnp.concatenate([x_ref[slot] for slot in cols], axis=0)
        kept = jnp.concatenate(
            [
                (lane >= 32 * part) & (lane < 32 * part + rank_ref[first + part])
                for part in range(8)
            ],
            axis=0,
        )
        right_proj = lax.dot_general(x_col, right, NT, preferred_element_type=F32)
        left_proj = lax.dot_general(x_row, left, NT, preferred_element_type=F32)
        right_proj = jnp.where(kept, right_proj, 0.0).astype(BF16)
        left_proj = jnp.where(kept, left_proj, 0.0).astype(BF16)
        return rows, cols, left, right, right_proj, left_proj

    def far_sums(first, count):
        sums = []
        for rows, cols, left, right, right_proj, left_proj in [
            far_project(first + at) for at in range(0, count, 8)
        ]:
            to_row = jnp.dot(right_proj, left, preferred_element_type=F32)
            to_col = jnp.dot(left_proj, right, preferred_element_type=F32)
            for part in range(8):
                sums.append((rows[part], to_row[16 * part : 16 * part + 16]))
                sums.append((cols[part], to_col[16 * part : 16 * part + 16]))
        return sums

    def add(sums):
        for slot, value in sums:
            acc_ref[slot] += value

    add(near_sums(kept_ref, 0, kept, 0))
    for quarter in range(QUARTERS):
        for copy in copies[quarter]:
            copy.wait()
        sums = far_sums(quarter * far_step, far_step)
        add(sums + near_sums(near_ref, quarter * near_step, near_step, kept))

    products = jnp.zeros((128, 128), F32)
    for at in range(slots // 8):
        here = slice(at * 8, at * 8 + 8)
        sums = acc_ref[here].astype(BF16)
        out_ref[here, 0:16, :] = sums[:, :, 0:128]
        out_ref[here, 16:32, :] = sums[:, :, 128:256]
        products = products + lax.dot_general(
            x_ref[here].reshape(128, 256),
            sums.reshape(128, 256),
            NT,
            preferred_element_type=F32,
        )
    tile = pack(fold(products) + small_ref[0], small_ref[1])

    def attach(at, carry):
        out_ref[pl.ds(at * 8, 8), 32:40, :] = jnp.broadcast_to(tile[None], (8, 8, 128))
        return carry

    lax.fori_loop(0, slots // 8, attach, 0)


def add_returned(leaf_ref, sums_ref, accs):
    def some(at, tiles):
        for part in range(16):
            owner = at * 16 + part
            leaf = leaf_ref[owner]
            acc_ref = accs[part % len(accs)]
            acc_ref[leaf, :, 0:128] += sums_ref[owner, 0:16, :].astype(F32)
            acc_ref[leaf, :, 128:256] += sums_ref[owner, 16:32, :].astype(F32)
            tiles = tiles + sums_ref[owner, 32:40, :].astype(F32)
        return tiles

    for acc_ref in accs[1:]:
        acc_ref[...] = jnp.zeros(acc_ref.shape, F32)
    tiles = lax.fori_loop(0, sums_ref.shape[0] // 16, some, jnp.zeros((8, 128), F32))
    return tiles, (accs[0][...] + accs[1][...]) + (accs[2][...] + accs[3][...])


def leaf_kernel(
    leaf_ref, sums_ref, base_ref, field_ref,
    residual_ref, image_ref, small_ref, message_ref,
    half_ref, stage_ref, acc_a, acc_b, acc_c, sems,
):
    image_ref[...] = base_ref[...]
    tiles, image = add_returned(leaf_ref, sums_ref, (image_ref, acc_a, acc_b, acc_c))
    curve, norm = unpack(tiles)
    step = solve(curve, norm)
    image_ref[...] = image
    image = image.reshape(128, 256)
    residual = field_ref[...].reshape(128, 256) - combine(image, kron_rows(step))
    half_ref[...] = residual.reshape(residual_ref.shape).astype(BF16)
    copies = fill(leaf_ref, half_ref, stage_ref, message_ref, sems)
    residual_ref[...] = residual.reshape(residual_ref.shape)
    small_ref[0] = from_columns(curve)
    small_ref[1] = norm
    small_ref[2] = step
    for copy in copies:
        copy.wait()


def final_kernel(
    leaf_ref, sums_ref, base_ref, field_ref, residual_ref, image_ref, small_ref, part_ref, steps_ref,
    solution_ref, out_ref, acc_ref, acc_a, acc_b, acc_c,
):
    acc_ref[...] = base_ref[...]
    tiles, returned = add_returned(leaf_ref, sums_ref, (acc_ref, acc_a, acc_b, acc_c))
    curve, next_norm = unpack(tiles)
    steps = [(steps_ref[step], steps_ref[16, step : step + 1]) for step in range(16)]
    coef = apply_factor(steps, next_norm)
    moved = product(columns(small_ref[0]), coef)
    moved = product(columns(coef.T[0:16]), moved)
    moved = columns(moved)
    step = solve([curve[at] - moved[at] for at in range(16)], next_norm)
    kron_coef = kron_rows(coef)
    residual = residual_ref[...].reshape(128, 256)
    direction = residual + combine(field_ref[...].reshape(128, 256), kron_coef)
    image = returned.reshape(128, 256) + combine(
        image_ref[...].reshape(128, 256), kron_coef
    )
    kron_step = kron_rows(step)
    answer = part_ref[...].reshape(128, 256) + combine(direction, kron_step)
    solution_ref[...] = answer.reshape(solution_ref.shape)
    out_ref[...] = (residual - combine(image, kron_step)).reshape(out_ref.shape)


def call(kernel, ins, outs, scratch, cost=None):
    kinds = {pltpu.HBM: HBM, pltpu.SMEM: TABLE}
    spaces = [kinds.get(getattr(out, "memory_space", None), VMEM) for out in outs]
    run = pl.pallas_call(
        kernel,
        out_shape=list(outs),
        in_specs=list(ins),
        out_specs=spaces,
        scratch_shapes=list(scratch),
        compiler_params=pltpu.CompilerParams(vmem_limit_bytes=24 * 1024 * 1024),
        cost_estimate=cost,
    )

    def placed(*values):
        return run(
            *(
                pltpu.with_memory_space_constraint(value, spec.memory_space)
                if spec is not VMEM
                else value
                for value, spec in zip(values, ins)
            )
        )

    return placed


def swap(values):
    return lax.all_to_all(values, AXES, split_axis=0, concat_axis=0, tiled=True)


def shards(
    right_sides,
    diag_shift,
    self_blocks,
    near_blocks,
    far_left,
    far_right,
    far_rank,
    send_leaf,
    block_pos,
):
    leaves, rhs, size = right_sides.shape
    slots = send_leaf.shape[1]
    targets = send_leaf.reshape(slots)
    whole = (leaves, rhs, size)
    message = (slots, rhs, size)
    local_cost = pl.CostEstimate(
        flops=4 * leaves * rhs * size * size, bytes_accessed=2 * leaves * size * size, transcendentals=0
    )
    send = call(
        send_kernel,
        [HBM, HBM],
        [pltpu.HBM(message, BF16)],
        [
            pltpu.SMEM((slots,), jnp.int32),
            pltpu.VMEM(whole, F32),
            pltpu.VMEM(whole, BF16),
            pltpu.VMEM(message, BF16),
            pltpu.SemaphoreType.DMA((6,)),
        ],
    )
    base = call(
        base_kernel,
        [VMEM, VMEM, HBM, HBM, HBM, HBM, HBM],
        [
            pltpu.VMEM(whole, F32),
            pltpu.VMEM((2, rhs, 128), F32),
            pltpu.VMEM((KEPT_NEAR, size, size), BF16),
            pltpu.SMEM((slots,), jnp.int32),
            pltpu.SMEM(far_rank.shape, jnp.int32),
            pltpu.SMEM(block_pos.shape, jnp.int32),
        ],
        [pltpu.VMEM(self_blocks.shape, BF16), pltpu.SemaphoreType.DMA((5,))],
        local_cost,
    )
    next_base = call(
        next_base_kernel,
        [KEPT, VMEM, HBM, KEPT, VMEM],
        [
            pltpu.VMEM(whole, F32),
            pltpu.VMEM((2, rhs, 128), F32),
            pltpu.VMEM(whole, F32),
            pltpu.VMEM((17, rhs, 128), F32),
        ],
        [pltpu.VMEM(self_blocks.shape, BF16), pltpu.SemaphoreType.DMA],
        local_cost,
    )
    owner = call(
        owner_kernel,
        [TABLE, TABLE, VMEM, KEPT, HBM, HBM, HBM, KEPT],
        [pltpu.VMEM((slots, 40, 128), BF16)],
        [
            pltpu.VMEM((near_blocks.shape[0] - KEPT_NEAR, size, size), BF16),
            pltpu.VMEM(far_left.shape, BF16),
            pltpu.VMEM(far_right.shape, BF16),
            pltpu.VMEM(message, F32),
            pltpu.SemaphoreType.DMA((QUARTERS, 3)),
        ],
    )
    leaf = call(
        leaf_kernel,
        [TABLE, VMEM, KEPT, VMEM],
        [
            pltpu.VMEM(whole, F32),
            pltpu.VMEM(whole, F32),
            pltpu.VMEM((3, rhs, 128), F32),
            pltpu.HBM(message, BF16),
        ],
        [
            pltpu.VMEM(whole, BF16),
            pltpu.VMEM(message, BF16),
            pltpu.VMEM(whole, F32),
            pltpu.VMEM(whole, F32),
            pltpu.VMEM(whole, F32),
            pltpu.SemaphoreType.DMA((4,)),
        ],
    )
    final = call(
        final_kernel,
        [TABLE, VMEM, KEPT, VMEM, KEPT, KEPT, KEPT, KEPT, KEPT],
        [jax.ShapeDtypeStruct(whole, F32), jax.ShapeDtypeStruct(whole, F32)],
        [pltpu.VMEM(whole, F32)] * 4,
    )

    with jax.named_scope("send"):
        (outgoing,) = send(targets, right_sides)
    incoming = swap(outgoing)
    with jax.named_scope("base"):
        base_image, small, kept, leaf_table, rank_table, at_table = base(
            right_sides, diag_shift, self_blocks, near_blocks, targets, far_rank, block_pos
        )
    with jax.named_scope("owner"):
        (sums,) = owner(
            rank_table, at_table, incoming, kept, near_blocks, far_left, far_right, small
        )
    back = swap(sums)
    with jax.named_scope("leaf"):
        residual, image, old, outgoing = leaf(leaf_table, back, base_image, right_sides)
    incoming = swap(outgoing)
    with jax.named_scope("base"):
        base_image, small, part, steps = next_base(
            residual, diag_shift, self_blocks, old, right_sides
        )
    with jax.named_scope("owner"):
        (sums,) = owner(
            rank_table, at_table, incoming, kept, near_blocks, far_left, far_right, small
        )
    back = swap(sums)
    with jax.named_scope("final"):
        answer, residual = final(
            leaf_table, back, base_image, right_sides, residual, image, old, part, steps
        )
    return (answer, residual)


def solution(mesh):
    split = P(AXES, None, None)
    placed = (
        split,
        P(AXES, None),
        split,
        split,
        split,
        split,
        P(AXES),
        split,
        P(None, AXES),
    )
    return jax.shard_map(
        shards, mesh=mesh, in_specs=placed, out_specs=(split, split), check_vma=False
    )
```

```python
import jax
import jax.numpy as jnp
from jax import lax
from jax.experimental import pallas as pl
from jax.experimental.pallas import tpu as pltpu
from jax.sharding import PartitionSpec as P

AXES = ("clus", "grp")
KEPT_NEAR = 16
QUARTERS = 4
HIGHEST = lax.Precision.HIGHEST
NT = (((1,), (1,)), ((), ()))
F32 = jnp.float32
BF16 = jnp.bfloat16

VMEM = pl.BlockSpec(memory_space=pltpu.VMEM)
HBM = pl.BlockSpec(memory_space=pltpu.HBM)
KEPT = pl.BlockSpec(memory_space=pltpu.VMEM)
TABLE = pl.BlockSpec(memory_space=pltpu.SMEM)


def iota(shape, dim):
    return lax.broadcasted_iota(jnp.int32, shape, dim)


def spread(values):
    values = values + pltpu.roll(values, 64, 1)
    values = values + pltpu.roll(values, 32, 1)
    return values + pltpu.roll(values, 16, 1)


def block_mask():
    return iota((128, 128), 0) // 16 == iota((128, 128), 1) // 16


def fold(products):
    kept = jnp.where(block_mask(), products, 0.0)
    total = kept[0:16]
    for part in range(1, 8):
        total = total + kept[16 * part : 16 * part + 16]
    return spread(total)


def kron_rows(coefs):
    tiled = jnp.concatenate([coefs] * 8, axis=0)
    return jnp.where(block_mask(), tiled, 0.0).T


def combine(field, kron):
    return jnp.dot(kron, field, precision=HIGHEST, preferred_element_type=F32)


def gram(left, right):
    return fold(lax.dot_general(left, right, NT, precision=HIGHEST, preferred_element_type=F32))


def columns(matrix):
    return [jnp.broadcast_to(matrix[:, at : at + 1], (16, 128)) for at in range(16)]


def factor(parts):
    row_at = iota((16, 128), 0)
    left = list(parts)
    steps = []
    for step in range(16):
        column = left[step]
        pivot = column[step : step + 1]
        scale = jnp.where(pivot > 0, 1.0 / pivot, jnp.nan)
        steps.append((column, scale))
        for later in range(step + 1, 16):
            scaled = left[later][step : step + 1] * scale
            left[later] = jnp.where(row_at == step, scaled, left[later] - column * scaled)
    return steps


def apply_factor(steps, target):
    row_at = iota((16, 128), 0)
    for step, (column, scale) in enumerate(steps):
        scaled = target[step : step + 1] * scale
        target = jnp.where(row_at == step, scaled, target - column * scaled)
    return target


def solve(parts, target):
    return apply_factor(factor(parts), target)


def product(left, right):
    total = left[0] * right[0:1]
    for at in range(1, 16):
        total = total + left[at] * right[at : at + 1]
    return total


def pack(first, second):
    group = iota((8, 128), 1) // 16
    tile = jnp.zeros((8, 128), F32)
    at = 0
    for matrix in (first, second):
        high = matrix.astype(BF16).astype(F32)
        low = matrix - high
        for piece in (high, low):
            for half in (piece[0:8], piece[8:16]):
                tile = jnp.where(group == at, half, tile)
                at += 1
    return tile.astype(BF16)


def unpack(tile):
    group = iota((8, 128), 1) // 16
    joined = tile + pltpu.roll(tile, 128 - 32, 1)
    first = [
        jnp.concatenate(
            [
                jnp.broadcast_to(joined[:, at : at + 1], (8, 128)),
                jnp.broadcast_to(joined[:, 16 + at : 17 + at], (8, 128)),
            ],
            axis=0,
        )
        for at in range(16)
    ]
    halves = [spread(jnp.where(group == at, joined, 0.0)) for at in (4, 5)]
    return first, jnp.concatenate(halves, axis=0)


def from_columns(parts):
    group = iota((16, 128), 1) % 16
    matrix = parts[0]
    for at in range(1, 16):
        matrix = jnp.where(group == at, parts[at], matrix)
    return matrix


def fill(leaf_ref, half_ref, message_ref):
    def some(at, carry):
        for inner in range(16):
            owner = at * 16 + inner
            message_ref[owner] = half_ref[leaf_ref[owner]]
        return carry

    lax.fori_loop(0, message_ref.shape[0] // 16, some, 0)


def send_kernel(
    leaf_hbm, rank_hbm, at_hbm, field_hbm, near_hbm,
    message_ref, leaf_ref, rank_ref, at_ref, kept_ref, field_ref, half_ref, sems,
):
    copies = [
        pltpu.make_async_copy(field_hbm, field_ref, sems.at[0]),
        pltpu.make_async_copy(leaf_hbm, leaf_ref, sems.at[1]),
        pltpu.make_async_copy(rank_hbm, rank_ref, sems.at[2]),
        pltpu.make_async_copy(at_hbm, at_ref, sems.at[3]),
        pltpu.make_async_copy(near_hbm.at[pl.ds(0, kept_ref.shape[0])], kept_ref, sems.at[4]),
    ]
    for copy in copies:
        copy.start()
    copies[0].wait()
    half_ref[...] = field_ref[...].astype(BF16)
    copies[1].wait()
    fill(leaf_ref, half_ref, message_ref)
    for copy in copies[2:]:
        copy.wait()


def local_product(field_ref, shift_ref, self_ref, base_ref):
    for leaf in range(field_ref.shape[0]):
        field = field_ref[leaf]
        half = field.astype(BF16)
        block = self_ref[leaf]
        total = shift_ref[leaf : leaf + 1, :] * field
        total = total + lax.dot_general(half, block, NT, preferred_element_type=F32)
        base_ref[leaf] = total + jnp.dot(half, block, preferred_element_type=F32)


def first_owner_kernel(
    rank_ref, at_ref, x_ref, kept_ref, near_hbm, left_hbm, right_hbm, self_hbm, field_ref, shift_ref,
    out_ref, base_ref, near_ref, left_ref, right_ref, self_ref, acc_ref, sems,
):
    kept = kept_ref.shape[0]
    near_step = near_ref.shape[0] // QUARTERS
    far_step = left_ref.shape[0] // QUARTERS
    copies = []
    for quarter in range(QUARTERS):
        near_from = quarter * near_step
        far_here = pl.ds(quarter * far_step, far_step)
        copies.append(
            [
                pltpu.make_async_copy(
                    near_hbm.at[pl.ds(kept + near_from, near_step)],
                    near_ref.at[pl.ds(near_from, near_step)],
                    sems.at[quarter, 0],
                ),
                pltpu.make_async_copy(left_hbm.at[far_here], left_ref.at[far_here], sems.at[quarter, 1]),
                pltpu.make_async_copy(right_hbm.at[far_here], right_ref.at[far_here], sems.at[quarter, 2]),
            ]
        )
        for copy in copies[quarter]:
            copy.start()
    self_copy = pltpu.make_async_copy(self_hbm, self_ref, sems.at[0, 3])
    self_copy.start()
    products = Products(rank_ref, at_ref, x_ref, left_ref, right_ref, kept + near_ref.shape[0], acc_ref)
    products.clear()
    products.add(products.near(kept_ref, 0, kept, 0))
    for quarter in range(QUARTERS):
        for copy in copies[quarter]:
            copy.wait()
        sums = products.far(quarter * far_step, far_step)
        products.add(sums + products.near(near_ref, quarter * near_step, near_step, kept))
    self_copy.wait()
    local_product(field_ref, shift_ref, self_ref, base_ref)
    finish(x_ref, acc_ref, field_ref, base_ref, out_ref)


def next_owner_kernel(
    rank_ref, at_ref, x_ref, near_ref, left_ref, right_ref, self_ref, field_ref, shift_ref, old_ref,
    out_ref, base_ref, steps_ref, acc_ref,
):
    near = near_ref.shape[0]
    near_step = near // QUARTERS
    far_step = left_ref.shape[0] // QUARTERS
    products = Products(rank_ref, at_ref, x_ref, left_ref, right_ref, near, acc_ref)
    products.clear()

    def some(quarter, carry):
        sums = products.far(quarter * far_step, far_step)
        products.add(sums + products.near(near_ref, quarter * near_step, near_step, 0))
        return carry

    lax.fori_loop(0, QUARTERS, some, 0)
    local_product(field_ref, shift_ref, self_ref, base_ref)
    for step, (column, scale) in enumerate(factor(columns(old_ref[1]))):
        steps_ref[step] = column
        steps_ref[16, step : step + 1] = scale
    finish(x_ref, acc_ref, field_ref, base_ref, out_ref)


class Products:
    def __init__(self, rank_ref, at_ref, x_ref, left_ref, right_ref, near_count, acc_ref):
        self.rank_ref = rank_ref
        self.at_ref = at_ref
        self.x_ref = x_ref
        self.left_ref = left_ref
        self.right_ref = right_ref
        self.near_count = near_count
        self.acc_ref = acc_ref

    def clear(self):
        def some(at, carry):
            self.acc_ref[pl.ds(at * 8, 8)] = jnp.zeros((8, 16, 256), F32)
            return carry

        lax.fori_loop(0, self.acc_ref.shape[0] // 8, some, 0)

    def add(self, sums):
        for slot, value in sums:
            self.acc_ref[slot] += value

    def near(self, block_ref, first, count, shift):
        sums = []
        for part in range(count):
            which = first + part
            row, col = self.at_ref[0, shift + which], self.at_ref[1, shift + which]
            block = block_ref[which]
            sums.append(
                (row, lax.dot_general(self.x_ref[col], block, NT, preferred_element_type=F32))
            )
            sums.append((col, jnp.dot(self.x_ref[row], block, preferred_element_type=F32)))
        return sums

    def project(self, first):
        lane = iota((16, 256), 1)
        left = self.left_ref[pl.ds(first, 8)].reshape(256, 256)
        right = self.right_ref[pl.ds(first, 8)].reshape(256, 256)
        rows = [self.at_ref[0, self.near_count + first + part] for part in range(8)]
        cols = [self.at_ref[1, self.near_count + first + part] for part in range(8)]
        x_row = jnp.concatenate([self.x_ref[slot] for slot in rows], axis=0)
        x_col = jnp.concatenate([self.x_ref[slot] for slot in cols], axis=0)
        kept = jnp.concatenate(
            [
                (lane >= 32 * part) & (lane < 32 * part + self.rank_ref[first + part])
                for part in range(8)
            ],
            axis=0,
        )
        right_proj = lax.dot_general(x_col, right, NT, preferred_element_type=F32)
        left_proj = lax.dot_general(x_row, left, NT, preferred_element_type=F32)
        right_proj = jnp.where(kept, right_proj, 0.0).astype(BF16)
        left_proj = jnp.where(kept, left_proj, 0.0).astype(BF16)
        return rows, cols, left, right, right_proj, left_proj

    def far(self, first, count):
        sums = []
        for rows, cols, left, right, right_proj, left_proj in [
            self.project(first + at) for at in range(0, count, 8)
        ]:
            to_row = jnp.dot(right_proj, left, preferred_element_type=F32)
            to_col = jnp.dot(left_proj, right, preferred_element_type=F32)
            for part in range(8):
                sums.append((rows[part], to_row[16 * part : 16 * part + 16]))
                sums.append((cols[part], to_col[16 * part : 16 * part + 16]))
        return sums


def finish(x_ref, acc_ref, field_ref, base_ref, out_ref):
    slots = x_ref.shape[0]
    fields = field_ref[...].reshape(128, 256)
    curve = gram(fields, base_ref[...].reshape(128, 256))
    norm = gram(fields, fields)
    products = jnp.zeros((128, 128), F32)
    for at in range(slots // 16):
        here = slice(at * 16, at * 16 + 16)
        sums = acc_ref[here].astype(BF16)
        out_ref[here, 0:16, :] = sums[:, :, 0:128]
        out_ref[here, 16:32, :] = sums[:, :, 128:256]
        pair = lax.dot_general(
            x_ref[here].reshape(256, 256),
            sums.reshape(256, 256),
            NT,
            preferred_element_type=F32,
        )
        products = products + (pair[0:128, 0:128] + pair[128:256, 128:256])
    tile = pack(fold(products) + curve, norm)

    def attach(at, carry):
        out_ref[pl.ds(at * 8, 8), 32:40, :] = jnp.broadcast_to(tile[None], (8, 8, 128))
        return carry

    lax.fori_loop(0, slots // 8, attach, 0)


def add_returned(leaf_ref, sums_ref, accs):
    def some(at, tiles):
        for part in range(16):
            owner = at * 16 + part
            leaf = leaf_ref[owner]
            acc_ref = accs[part % len(accs)]
            acc_ref[leaf, :, 0:128] += sums_ref[owner, 0:16, :].astype(F32)
            acc_ref[leaf, :, 128:256] += sums_ref[owner, 16:32, :].astype(F32)
            tiles = tiles + sums_ref[owner, 32:40, :].astype(F32)
        return tiles

    for acc_ref in accs[1:]:
        acc_ref[...] = jnp.zeros(acc_ref.shape, F32)
    tiles = lax.fori_loop(0, sums_ref.shape[0] // 16, some, jnp.zeros((8, 128), F32))
    return tiles, (accs[0][...] + accs[1][...]) + (accs[2][...] + accs[3][...])


def leaf_kernel(
    leaf_ref, sums_ref, base_ref, field_ref,
    residual_ref, image_ref, small_ref, message_ref,
    half_ref, acc_a, acc_b, acc_c,
):
    image_ref[...] = base_ref[...]
    tiles, image = add_returned(leaf_ref, sums_ref, (image_ref, acc_a, acc_b, acc_c))
    curve, norm = unpack(tiles)
    step = solve(curve, norm)
    image_ref[...] = image
    image = image.reshape(128, 256)
    residual = field_ref[...].reshape(128, 256) - combine(image, kron_rows(step))
    half_ref[...] = residual.reshape(residual_ref.shape).astype(BF16)
    fill(leaf_ref, half_ref, message_ref)
    residual_ref[...] = residual.reshape(residual_ref.shape)
    small_ref[0] = from_columns(curve)
    small_ref[1] = norm
    small_ref[2] = step


def final_kernel(
    leaf_ref, sums_ref, base_ref, field_ref, residual_ref, image_ref, small_ref, steps_ref,
    solution_ref, out_ref, acc_ref, acc_a, acc_b, acc_c,
):
    acc_ref[...] = base_ref[...]
    tiles, returned = add_returned(leaf_ref, sums_ref, (acc_ref, acc_a, acc_b, acc_c))
    curve, next_norm = unpack(tiles)
    steps = [(steps_ref[step], steps_ref[16, step : step + 1]) for step in range(16)]
    coef = apply_factor(steps, next_norm)
    moved = product(columns(small_ref[0]), coef)
    moved = product(columns(coef.T[0:16]), moved)
    moved = columns(moved)
    step = solve([curve[at] - moved[at] for at in range(16)], next_norm)
    kron_coef = kron_rows(coef)
    part = combine(field_ref[...].reshape(128, 256), kron_rows(small_ref[2]))
    residual = residual_ref[...].reshape(128, 256)
    direction = residual + combine(field_ref[...].reshape(128, 256), kron_coef)
    image = returned.reshape(128, 256) + combine(
        image_ref[...].reshape(128, 256), kron_coef
    )
    kron_step = kron_rows(step)
    answer = part + combine(direction, kron_step)
    solution_ref[...] = answer.reshape(solution_ref.shape)
    out_ref[...] = (residual - combine(image, kron_step)).reshape(out_ref.shape)


def call(kernel, ins, outs, scratch, cost=None):
    kinds = {pltpu.HBM: HBM, pltpu.SMEM: TABLE}
    spaces = [kinds.get(getattr(out, "memory_space", None), VMEM) for out in outs]
    run = pl.pallas_call(
        kernel,
        out_shape=list(outs),
        in_specs=list(ins),
        out_specs=spaces,
        scratch_shapes=list(scratch),
        compiler_params=pltpu.CompilerParams(vmem_limit_bytes=24 * 1024 * 1024),
        cost_estimate=cost,
    )

    def placed(*values):
        return run(
            *(
                pltpu.with_memory_space_constraint(value, spec.memory_space)
                if spec is not VMEM
                else value
                for value, spec in zip(values, ins)
            )
        )

    return placed


def swap(values):
    return lax.all_to_all(values, AXES, split_axis=0, concat_axis=0, tiled=True)


def shards(
    right_sides,
    diag_shift,
    self_blocks,
    near_blocks,
    far_left,
    far_right,
    far_rank,
    send_leaf,
    block_pos,
):
    leaves, rhs, size = right_sides.shape
    slots = send_leaf.shape[1]
    targets = send_leaf.reshape(slots)
    whole = (leaves, rhs, size)
    message = (slots, rhs, size)
    tables = [
        pltpu.SMEM((slots,), jnp.int32),
        pltpu.SMEM(far_rank.shape, jnp.int32),
        pltpu.SMEM(block_pos.shape, jnp.int32),
    ]
    send = call(
        send_kernel,
        [HBM, HBM, HBM, HBM, HBM],
        [jax.ShapeDtypeStruct(message, BF16)]
        + tables
        + [pltpu.VMEM((KEPT_NEAR, size, size), BF16)],
        [pltpu.VMEM(whole, F32), pltpu.VMEM(whole, BF16), pltpu.SemaphoreType.DMA((5,))],
    )
    owner_outs = [pltpu.VMEM((slots, 40, 128), BF16), pltpu.VMEM(whole, F32)]
    owner = call(
        first_owner_kernel,
        [TABLE, TABLE, VMEM, KEPT, HBM, HBM, HBM, HBM, VMEM, VMEM],
        owner_outs,
        [
            pltpu.VMEM((near_blocks.shape[0] - KEPT_NEAR, size, size), BF16),
            pltpu.VMEM(far_left.shape, BF16),
            pltpu.VMEM(far_right.shape, BF16),
            pltpu.VMEM(self_blocks.shape, BF16),
            pltpu.VMEM(message, F32),
            pltpu.SemaphoreType.DMA((QUARTERS, 4)),
        ],
    )
    next_owner = call(
        next_owner_kernel,
        [TABLE, TABLE] + [VMEM] * 7 + [KEPT],
        owner_outs + [pltpu.VMEM((17, rhs, 128), F32)],
        [pltpu.VMEM(message, F32)],
    )
    leaf = call(
        leaf_kernel,
        [TABLE, VMEM, KEPT, VMEM],
        [
            pltpu.VMEM(whole, F32),
            pltpu.VMEM(whole, F32),
            pltpu.VMEM((3, rhs, 128), F32),
            jax.ShapeDtypeStruct(message, BF16),
        ],
        [pltpu.VMEM(whole, BF16)] + [pltpu.VMEM(whole, F32)] * 3,
    )
    final = call(
        final_kernel,
        [TABLE, VMEM, KEPT, VMEM, KEPT, KEPT, KEPT, KEPT],
        [jax.ShapeDtypeStruct(whole, F32), jax.ShapeDtypeStruct(whole, F32)],
        [pltpu.VMEM(whole, F32)] * 4,
    )
    stored = (near_blocks, far_left, far_right, self_blocks)

    with jax.named_scope("send"):
        outgoing, leaf_table, rank_table, at_table, kept = send(
            targets, far_rank, block_pos, right_sides, near_blocks
        )
    incoming = swap(outgoing)
    with jax.named_scope("owner"):
        sums, base_image = owner(
            rank_table, at_table, incoming, kept, *stored, right_sides, diag_shift
        )
    back = swap(sums)
    with jax.named_scope("leaf"):
        residual, image, old, outgoing = leaf(leaf_table, back, base_image, right_sides)
    incoming = swap(outgoing)
    with jax.named_scope("owner"):
        sums, base_image, steps = next_owner(
            rank_table, at_table, incoming, *stored, residual, diag_shift, old
        )
    back = swap(sums)
    with jax.named_scope("final"):
        answer, residual = final(
            leaf_table, back, base_image, right_sides, residual, image, old, steps
        )
    return (answer, residual)


def solution(mesh):
    split = P(AXES, None, None)
    placed = (
        split,
        P(AXES, None),
        split,
        split,
        split,
        split,
        P(AXES),
        split,
        P(None, AXES),
    )
    return jax.shard_map(
        shards, mesh=mesh, in_specs=placed, out_specs=(split, split), check_vma=False
    )
```

```python
import jax
import jax.numpy as jnp
from jax import lax
from jax.experimental import pallas as pl
from jax.experimental.pallas import tpu as pltpu
from jax.sharding import PartitionSpec as P

AXES = ("clus", "grp")
KEPT_NEAR = 4
QUARTERS = 4
HIGHEST = lax.Precision.HIGHEST
NT = (((1,), (1,)), ((), ()))
F32 = jnp.float32
BF16 = jnp.bfloat16

VMEM = pl.BlockSpec(memory_space=pltpu.VMEM)
HBM = pl.BlockSpec(memory_space=pltpu.HBM)
KEPT = pl.BlockSpec(memory_space=pltpu.VMEM)
TABLE = pl.BlockSpec(memory_space=pltpu.SMEM)


def iota(shape, dim):
    return lax.broadcasted_iota(jnp.int32, shape, dim)


def spread(values):
    values = values + pltpu.roll(values, 64, 1)
    values = values + pltpu.roll(values, 32, 1)
    return values + pltpu.roll(values, 16, 1)


def block_mask():
    return iota((128, 128), 0) // 16 == iota((128, 128), 1) // 16


def fold(products):
    kept = jnp.where(block_mask(), products, 0.0)
    total = kept[0:16]
    for part in range(1, 8):
        total = total + kept[16 * part : 16 * part + 16]
    return spread(total)


def kron_rows(coefs):
    tiled = jnp.concatenate([coefs] * 8, axis=0)
    return jnp.where(block_mask(), tiled, 0.0).T


def combine(field, kron):
    return jnp.dot(kron, field, precision=HIGHEST, preferred_element_type=F32)


def gram(left, right):
    return fold(lax.dot_general(left, right, NT, precision=HIGHEST, preferred_element_type=F32))


def columns(matrix):
    return [jnp.broadcast_to(matrix[:, at : at + 1], (16, 128)) for at in range(16)]


def factor(parts):
    row_at = iota((16, 128), 0)
    left = list(parts)
    steps = []
    for step in range(16):
        column = left[step]
        pivot = column[step : step + 1]
        scale = jnp.where(pivot > 0, 1.0 / pivot, jnp.nan)
        steps.append((column, scale))
        for later in range(step + 1, 16):
            scaled = left[later][step : step + 1] * scale
            left[later] = jnp.where(row_at == step, scaled, left[later] - column * scaled)
    return steps


def apply_factor(steps, target):
    row_at = iota((16, 128), 0)
    for step, (column, scale) in enumerate(steps):
        scaled = target[step : step + 1] * scale
        target = jnp.where(row_at == step, scaled, target - column * scaled)
    return target


def solve(parts, target):
    return apply_factor(factor(parts), target)


def product(left, right):
    total = left[0] * right[0:1]
    for at in range(1, 16):
        total = total + left[at] * right[at : at + 1]
    return total


def pack(first, second):
    group = iota((8, 128), 1) // 16
    tile = jnp.zeros((8, 128), F32)
    at = 0
    for matrix in (first, second):
        high = matrix.astype(BF16).astype(F32)
        low = matrix - high
        for piece in (high, low):
            for half in (piece[0:8], piece[8:16]):
                tile = jnp.where(group == at, half, tile)
                at += 1
    return tile.astype(BF16)


def unpack(tile):
    group = iota((8, 128), 1) // 16
    joined = tile + pltpu.roll(tile, 128 - 32, 1)
    first = [
        jnp.concatenate(
            [
                jnp.broadcast_to(joined[:, at : at + 1], (8, 128)),
                jnp.broadcast_to(joined[:, 16 + at : 17 + at], (8, 128)),
            ],
            axis=0,
        )
        for at in range(16)
    ]
    halves = [spread(jnp.where(group == at, joined, 0.0)) for at in (4, 5)]
    return first, jnp.concatenate(halves, axis=0)


def from_columns(parts):
    group = iota((16, 128), 1) % 16
    matrix = parts[0]
    for at in range(1, 16):
        matrix = jnp.where(group == at, parts[at], matrix)
    return matrix


def fill(leaf_ref, half_ref, message_ref):
    def some(at, carry):
        for inner in range(16):
            owner = at * 16 + inner
            message_ref[owner] = half_ref[leaf_ref[owner]]
        return carry

    lax.fori_loop(0, message_ref.shape[0] // 16, some, 0)


def send_kernel(
    leaf_hbm, rank_hbm, at_hbm, field_hbm, near_hbm,
    message_ref, leaf_ref, rank_ref, at_ref, kept_ref, field_ref, half_ref, sems,
):
    copies = [
        pltpu.make_async_copy(field_hbm, field_ref, sems.at[0]),
        pltpu.make_async_copy(leaf_hbm, leaf_ref, sems.at[1]),
        pltpu.make_async_copy(rank_hbm, rank_ref, sems.at[2]),
        pltpu.make_async_copy(at_hbm, at_ref, sems.at[3]),
        pltpu.make_async_copy(near_hbm.at[pl.ds(0, kept_ref.shape[0])], kept_ref, sems.at[4]),
    ]
    for copy in copies:
        copy.start()
    copies[0].wait()
    half_ref[...] = field_ref[...].astype(BF16)
    copies[1].wait()
    fill(leaf_ref, half_ref, message_ref)
    for copy in copies[2:]:
        copy.wait()


def local_product(field_ref, shift_ref, self_ref, base_ref):
    for leaf in range(field_ref.shape[0]):
        field = field_ref[leaf]
        half = field.astype(BF16)
        block = self_ref[leaf]
        total = shift_ref[leaf : leaf + 1, :] * field
        total = total + lax.dot_general(half, block, NT, preferred_element_type=F32)
        base_ref[leaf] = total + jnp.dot(half, block, preferred_element_type=F32)


def first_owner_kernel(
    rank_ref, at_ref, x_ref, kept_ref, near_hbm, left_ref, right_ref, self_hbm, field_ref, shift_ref,
    out_ref, base_ref, near_ref, self_ref, acc_ref, sems,
):
    kept = kept_ref.shape[0]
    kept_step = kept // QUARTERS
    far_step = left_ref.shape[0] // QUARTERS
    rest = near_ref.shape[0]
    near_copy = pltpu.make_async_copy(near_hbm.at[pl.ds(kept, rest)], near_ref, sems.at[0])
    self_copy = pltpu.make_async_copy(self_hbm, self_ref, sems.at[1])
    near_copy.start()
    self_copy.start()
    products = Products(rank_ref, at_ref, x_ref, left_ref, right_ref, kept + rest, acc_ref)
    products.clear()
    for quarter in range(QUARTERS):
        sums = products.far(quarter * far_step, far_step)
        products.add(sums + products.near(kept_ref, quarter * kept_step, kept_step, 0))
    near_copy.wait()
    self_copy.wait()
    products.add(products.near(near_ref, 0, rest, kept))
    local_product(field_ref, shift_ref, self_ref, base_ref)
    finish(x_ref, acc_ref, field_ref, base_ref, out_ref)


def next_owner_kernel(
    rank_ref, at_ref, x_ref, near_ref, left_ref, right_ref, self_ref, field_ref, shift_ref, old_ref,
    out_ref, base_ref, steps_ref, acc_ref,
):
    near = near_ref.shape[0]
    near_step = near // QUARTERS
    far_step = left_ref.shape[0] // QUARTERS
    products = Products(rank_ref, at_ref, x_ref, left_ref, right_ref, near, acc_ref)
    products.clear()

    for quarter in range(QUARTERS):
        sums = products.far(quarter * far_step, far_step)
        products.add(sums + products.near(near_ref, quarter * near_step, near_step, 0))
    local_product(field_ref, shift_ref, self_ref, base_ref)
    for step, (column, scale) in enumerate(factor(columns(old_ref[1]))):
        steps_ref[step] = column
        steps_ref[16, step : step + 1] = scale
    finish(x_ref, acc_ref, field_ref, base_ref, out_ref)


class Products:
    def __init__(self, rank_ref, at_ref, x_ref, left_ref, right_ref, near_count, acc_ref):
        self.rank_ref = rank_ref
        self.at_ref = at_ref
        self.x_ref = x_ref
        self.left_ref = left_ref
        self.right_ref = right_ref
        self.near_count = near_count
        self.acc_ref = acc_ref

    def clear(self):
        def some(at, carry):
            self.acc_ref[pl.ds(at * 8, 8)] = jnp.zeros((8, 16, 256), F32)
            return carry

        lax.fori_loop(0, self.acc_ref.shape[0] // 8, some, 0)

    def add(self, sums):
        for slot, value in sums:
            self.acc_ref[slot] += value

    def near(self, block_ref, first, count, shift):
        sums = []
        for part in range(count):
            which = first + part
            row, col = self.at_ref[0, shift + which], self.at_ref[1, shift + which]
            block = block_ref[which]
            sums.append(
                (row, lax.dot_general(self.x_ref[col], block, NT, preferred_element_type=F32))
            )
            sums.append((col, jnp.dot(self.x_ref[row], block, preferred_element_type=F32)))
        return sums

    def project(self, first):
        lane = iota((16, 256), 1)
        left = self.left_ref[pl.ds(first, 8)].reshape(256, 256)
        right = self.right_ref[pl.ds(first, 8)].reshape(256, 256)
        rows = [self.at_ref[0, self.near_count + first + part] for part in range(8)]
        cols = [self.at_ref[1, self.near_count + first + part] for part in range(8)]
        x_row = jnp.concatenate([self.x_ref[slot] for slot in rows], axis=0)
        x_col = jnp.concatenate([self.x_ref[slot] for slot in cols], axis=0)
        kept = jnp.concatenate(
            [
                (lane >= 32 * part) & (lane < 32 * part + self.rank_ref[first + part])
                for part in range(8)
            ],
            axis=0,
        )
        right_proj = lax.dot_general(x_col, right, NT, preferred_element_type=F32)
        left_proj = lax.dot_general(x_row, left, NT, preferred_element_type=F32)
        right_proj = jnp.where(kept, right_proj, 0.0).astype(BF16)
        left_proj = jnp.where(kept, left_proj, 0.0).astype(BF16)
        return rows, cols, left, right, right_proj, left_proj

    def far(self, first, count):
        sums = []
        for rows, cols, left, right, right_proj, left_proj in [
            self.project(first + at) for at in range(0, count, 8)
        ]:
            to_row = jnp.dot(right_proj, left, preferred_element_type=F32)
            to_col = jnp.dot(left_proj, right, preferred_element_type=F32)
            for part in range(8):
                sums.append((rows[part], to_row[16 * part : 16 * part + 16]))
                sums.append((cols[part], to_col[16 * part : 16 * part + 16]))
        return sums


def finish(x_ref, acc_ref, field_ref, base_ref, out_ref):
    slots = x_ref.shape[0]
    fields = field_ref[...].reshape(128, 256)
    curve = gram(fields, base_ref[...].reshape(128, 256))
    norm = gram(fields, fields)
    products = jnp.zeros((128, 128), F32)
    for at in range(slots // 16):
        here = slice(at * 16, at * 16 + 16)
        sums = acc_ref[here].astype(BF16)
        out_ref[here, 0:16, :] = sums[:, :, 0:128]
        out_ref[here, 16:32, :] = sums[:, :, 128:256]
        pair = lax.dot_general(
            x_ref[here].reshape(256, 256),
            sums.reshape(256, 256),
            NT,
            preferred_element_type=F32,
        )
        products = products + (pair[0:128, 0:128] + pair[128:256, 128:256])
    tile = pack(fold(products) + curve, norm)

    def attach(at, carry):
        out_ref[pl.ds(at * 8, 8), 32:40, :] = jnp.broadcast_to(tile[None], (8, 8, 128))
        return carry

    lax.fori_loop(0, slots // 8, attach, 0)


def add_returned(leaf_ref, sums_ref, accs):
    def some(at, tiles):
        for part in range(16):
            owner = at * 16 + part
            leaf = leaf_ref[owner]
            acc_ref = accs[part % len(accs)]
            acc_ref[leaf, :, 0:128] += sums_ref[owner, 0:16, :].astype(F32)
            acc_ref[leaf, :, 128:256] += sums_ref[owner, 16:32, :].astype(F32)
            tiles = tiles + sums_ref[owner, 32:40, :].astype(F32)
        return tiles

    for acc_ref in accs[1:]:
        acc_ref[...] = jnp.zeros(acc_ref.shape, F32)
    tiles = lax.fori_loop(0, sums_ref.shape[0] // 16, some, jnp.zeros((8, 128), F32))
    return tiles, (accs[0][...] + accs[1][...]) + (accs[2][...] + accs[3][...])


def leaf_kernel(
    leaf_ref, sums_ref, base_ref, field_ref,
    residual_ref, image_ref, small_ref, message_ref,
    half_ref, acc_a, acc_b, acc_c,
):
    image_ref[...] = base_ref[...]
    tiles, image = add_returned(leaf_ref, sums_ref, (image_ref, acc_a, acc_b, acc_c))
    curve, norm = unpack(tiles)
    step = solve(curve, norm)
    image_ref[...] = image
    image = image.reshape(128, 256)
    residual = field_ref[...].reshape(128, 256) - combine(image, kron_rows(step))
    half_ref[...] = residual.reshape(residual_ref.shape).astype(BF16)
    fill(leaf_ref, half_ref, message_ref)
    residual_ref[...] = residual.reshape(residual_ref.shape)
    small_ref[0] = from_columns(curve)
    small_ref[1] = norm
    small_ref[2] = step


def final_kernel(
    leaf_ref, sums_ref, base_ref, field_ref, residual_ref, image_ref, small_ref, steps_ref,
    solution_ref, out_ref, acc_ref, acc_a, acc_b, acc_c,
):
    acc_ref[...] = base_ref[...]
    tiles, returned = add_returned(leaf_ref, sums_ref, (acc_ref, acc_a, acc_b, acc_c))
    curve, next_norm = unpack(tiles)
    steps = [(steps_ref[step], steps_ref[16, step : step + 1]) for step in range(16)]
    coef = apply_factor(steps, next_norm)
    moved = product(columns(small_ref[0]), coef)
    moved = product(columns(coef.T[0:16]), moved)
    moved = columns(moved)
    step = solve([curve[at] - moved[at] for at in range(16)], next_norm)
    kron_coef = kron_rows(coef)
    part = combine(field_ref[...].reshape(128, 256), kron_rows(small_ref[2]))
    residual = residual_ref[...].reshape(128, 256)
    direction = residual + combine(field_ref[...].reshape(128, 256), kron_coef)
    image = returned.reshape(128, 256) + combine(
        image_ref[...].reshape(128, 256), kron_coef
    )
    kron_step = kron_rows(step)
    answer = part + combine(direction, kron_step)
    solution_ref[...] = answer.reshape(solution_ref.shape)
    out_ref[...] = (residual - combine(image, kron_step)).reshape(out_ref.shape)


def call(kernel, ins, outs, scratch, cost=None):
    kinds = {pltpu.HBM: HBM, pltpu.SMEM: TABLE}
    spaces = [kinds.get(getattr(out, "memory_space", None), VMEM) for out in outs]
    run = pl.pallas_call(
        kernel,
        out_shape=list(outs),
        in_specs=list(ins),
        out_specs=spaces,
        scratch_shapes=list(scratch),
        compiler_params=pltpu.CompilerParams(vmem_limit_bytes=24 * 1024 * 1024),
        cost_estimate=cost,
    )

    def placed(*values):
        return run(
            *(
                pltpu.with_memory_space_constraint(value, spec.memory_space)
                if spec is not VMEM
                else value
                for value, spec in zip(values, ins)
            )
        )

    return placed


def swap(values):
    return lax.all_to_all(values, AXES, split_axis=0, concat_axis=0, tiled=True)


def shards(
    right_sides,
    diag_shift,
    self_blocks,
    near_blocks,
    far_left,
    far_right,
    far_rank,
    send_leaf,
    block_pos,
):
    leaves, rhs, size = right_sides.shape
    slots = send_leaf.shape[1]
    targets = send_leaf.reshape(slots)
    whole = (leaves, rhs, size)
    message = (slots, rhs, size)
    tables = [
        pltpu.SMEM((slots,), jnp.int32),
        pltpu.SMEM(far_rank.shape, jnp.int32),
        pltpu.SMEM(block_pos.shape, jnp.int32),
    ]
    send = call(
        send_kernel,
        [HBM, HBM, HBM, HBM, HBM],
        [jax.ShapeDtypeStruct(message, BF16)]
        + tables
        + [pltpu.VMEM((KEPT_NEAR, size, size), BF16)],
        [pltpu.VMEM(whole, F32), pltpu.VMEM(whole, BF16), pltpu.SemaphoreType.DMA((5,))],
    )
    owner_outs = [pltpu.VMEM((slots, 40, 128), BF16), pltpu.VMEM(whole, F32)]
    owner = call(
        first_owner_kernel,
        [TABLE, TABLE, VMEM, KEPT, HBM, VMEM, VMEM, HBM, VMEM, VMEM],
        owner_outs,
        [
            pltpu.VMEM((near_blocks.shape[0] - KEPT_NEAR, size, size), BF16),
            pltpu.VMEM(self_blocks.shape, BF16),
            pltpu.VMEM(message, F32),
            pltpu.SemaphoreType.DMA((2,)),
        ],
    )
    next_owner = call(
        next_owner_kernel,
        [TABLE, TABLE] + [VMEM] * 7 + [KEPT],
        owner_outs + [pltpu.VMEM((17, rhs, 128), F32)],
        [pltpu.VMEM(message, F32)],
    )
    leaf = call(
        leaf_kernel,
        [TABLE, VMEM, KEPT, VMEM],
        [
            pltpu.VMEM(whole, F32),
            pltpu.VMEM(whole, F32),
            pltpu.VMEM((3, rhs, 128), F32),
            jax.ShapeDtypeStruct(message, BF16),
        ],
        [pltpu.VMEM(whole, BF16)] + [pltpu.VMEM(whole, F32)] * 3,
    )
    final = call(
        final_kernel,
        [TABLE, VMEM, KEPT, VMEM, KEPT, KEPT, KEPT, KEPT],
        [jax.ShapeDtypeStruct(whole, F32), jax.ShapeDtypeStruct(whole, F32)],
        [pltpu.VMEM(whole, F32)] * 4,
    )
    stored = (near_blocks, far_left, far_right, self_blocks)

    with jax.named_scope("send"):
        outgoing, leaf_table, rank_table, at_table, kept = send(
            targets, far_rank, block_pos, right_sides, near_blocks
        )
    incoming = swap(outgoing)
    with jax.named_scope("owner"):
        sums, base_image = owner(
            rank_table, at_table, incoming, kept, *stored, right_sides, diag_shift
        )
    back = swap(sums)
    with jax.named_scope("leaf"):
        residual, image, old, outgoing = leaf(leaf_table, back, base_image, right_sides)
    incoming = swap(outgoing)
    with jax.named_scope("owner"):
        sums, base_image, steps = next_owner(
            rank_table, at_table, incoming, *stored, residual, diag_shift, old
        )
    back = swap(sums)
    with jax.named_scope("final"):
        answer, residual = final(
            leaf_table, back, base_image, right_sides, residual, image, old, steps
        )
    return (answer, residual)


def solution(mesh):
    split = P(AXES, None, None)
    placed = (
        split,
        P(AXES, None),
        split,
        split,
        split,
        split,
        P(AXES),
        split,
        P(None, AXES),
    )
    return jax.shard_map(
        shards, mesh=mesh, in_specs=placed, out_specs=(split, split), check_vma=False
    )
```

```python
import jax
import jax.numpy as jnp
from jax import lax
from jax.experimental import pallas as pl
from jax.experimental.pallas import tpu as pltpu
from jax.sharding import PartitionSpec as P

AXES = ("clus", "grp")
KEPT_NEAR = 4
QUARTERS = 4
HIGHEST = lax.Precision.HIGHEST
NT = (((1,), (1,)), ((), ()))
F32 = jnp.float32
BF16 = jnp.bfloat16

VMEM = pl.BlockSpec(memory_space=pltpu.VMEM)
HBM = pl.BlockSpec(memory_space=pltpu.HBM)
KEPT = pl.BlockSpec(memory_space=pltpu.VMEM)
TABLE = pl.BlockSpec(memory_space=pltpu.SMEM)


def iota(shape, dim):
    return lax.broadcasted_iota(jnp.int32, shape, dim)


def spread(values):
    values = values + pltpu.roll(values, 64, 1)
    values = values + pltpu.roll(values, 32, 1)
    return values + pltpu.roll(values, 16, 1)


def block_mask():
    return iota((128, 128), 0) // 16 == iota((128, 128), 1) // 16


def fold(products):
    kept = jnp.where(block_mask(), products, 0.0)
    total = kept[0:16]
    for part in range(1, 8):
        total = total + kept[16 * part : 16 * part + 16]
    return spread(total)


def kron_rows(coefs):
    tiled = jnp.concatenate([coefs] * 8, axis=0)
    return jnp.where(block_mask(), tiled, 0.0).T


def combine(field, kron):
    return jnp.dot(kron, field, precision=HIGHEST, preferred_element_type=F32)


def pieces(values):
    high = values.astype(BF16)
    return high, (values - high.astype(F32)).astype(BF16)


def combine_pieces(field, kron):
    high, low = pieces(field)
    kron_high, kron_low = pieces(kron)
    main = jnp.dot(
        jnp.concatenate([kron_high, kron_low], axis=0), high, preferred_element_type=F32
    )
    rest = jnp.dot(kron_high, low, preferred_element_type=F32)
    return main[0:128] + (main[128:256] + rest)


def gram(left, right):
    return fold(lax.dot_general(left, right, NT, precision=HIGHEST, preferred_element_type=F32))


def columns(matrix):
    return [jnp.broadcast_to(matrix[:, at : at + 1], (16, 128)) for at in range(16)]


def factor(parts):
    row_at = iota((16, 128), 0)
    left = list(parts)
    steps = []
    for step in range(16):
        column = left[step]
        pivot = column[step : step + 1]
        scale = jnp.where(pivot > 0, 1.0 / pivot, jnp.nan)
        steps.append((column, scale))
        for later in range(step + 1, 16):
            scaled = left[later][step : step + 1] * scale
            left[later] = jnp.where(row_at == step, scaled, left[later] - column * scaled)
    return steps


def apply_factor(steps, target):
    row_at = iota((16, 128), 0)
    for step, (column, scale) in enumerate(steps):
        scaled = target[step : step + 1] * scale
        target = jnp.where(row_at == step, scaled, target - column * scaled)
    return target


def solve(parts, target):
    return apply_factor(factor(parts), target)


def product(left, right):
    total = left[0] * right[0:1]
    for at in range(1, 16):
        total = total + left[at] * right[at : at + 1]
    return total


def pack(first, second):
    group = iota((8, 128), 1) // 16
    tile = jnp.zeros((8, 128), F32)
    at = 0
    for matrix in (first, second):
        high = matrix.astype(BF16).astype(F32)
        low = matrix - high
        for piece in (high, low):
            for half in (piece[0:8], piece[8:16]):
                tile = jnp.where(group == at, half, tile)
                at += 1
    return tile.astype(BF16)


def unpack(tile):
    group = iota((8, 128), 1) // 16
    joined = tile + pltpu.roll(tile, 128 - 32, 1)
    first = [
        jnp.concatenate(
            [
                jnp.broadcast_to(joined[:, at : at + 1], (8, 128)),
                jnp.broadcast_to(joined[:, 16 + at : 17 + at], (8, 128)),
            ],
            axis=0,
        )
        for at in range(16)
    ]
    halves = [spread(jnp.where(group == at, joined, 0.0)) for at in (4, 5)]
    return first, jnp.concatenate(halves, axis=0)


def from_columns(parts):
    group = iota((16, 128), 1) % 16
    matrix = parts[0]
    for at in range(1, 16):
        matrix = jnp.where(group == at, parts[at], matrix)
    return matrix


def fill(leaf_ref, half_ref, message_ref):
    def some(at, carry):
        for inner in range(16):
            owner = at * 16 + inner
            message_ref[owner] = half_ref[leaf_ref[owner]]
        return carry

    lax.fori_loop(0, message_ref.shape[0] // 16, some, 0)


def send_kernel(
    leaf_hbm, rank_hbm, at_hbm, field_hbm, near_hbm,
    message_ref, leaf_ref, rank_ref, at_ref, kept_ref, field_ref, half_ref, sems,
):
    copies = [
        pltpu.make_async_copy(field_hbm, field_ref, sems.at[0]),
        pltpu.make_async_copy(leaf_hbm, leaf_ref, sems.at[1]),
        pltpu.make_async_copy(rank_hbm, rank_ref, sems.at[2]),
        pltpu.make_async_copy(at_hbm, at_ref, sems.at[3]),
        pltpu.make_async_copy(near_hbm.at[pl.ds(0, kept_ref.shape[0])], kept_ref, sems.at[4]),
    ]
    for copy in copies:
        copy.start()
    copies[0].wait()
    half_ref[...] = field_ref[...].astype(BF16)
    copies[1].wait()
    fill(leaf_ref, half_ref, message_ref)
    for copy in copies[2:]:
        copy.wait()


def local_product(field_ref, shift_ref, self_ref, base_ref):
    for leaf in range(field_ref.shape[0]):
        field = field_ref[leaf]
        half = field.astype(BF16)
        block = self_ref[leaf]
        total = shift_ref[leaf : leaf + 1, :] * field
        total = total + lax.dot_general(half, block, NT, preferred_element_type=F32)
        base_ref[leaf] = total + jnp.dot(half, block, preferred_element_type=F32)


def first_owner_kernel(
    rank_ref, at_ref, x_ref, kept_ref, near_hbm, left_ref, right_ref, self_hbm, field_ref, shift_ref,
    out_ref, base_ref, near_ref, self_ref, acc_ref, sems,
):
    kept = kept_ref.shape[0]
    kept_step = kept // QUARTERS
    far_step = left_ref.shape[0] // QUARTERS
    rest = near_ref.shape[0]
    near_copy = pltpu.make_async_copy(near_hbm.at[pl.ds(kept, rest)], near_ref, sems.at[0])
    self_copy = pltpu.make_async_copy(self_hbm, self_ref, sems.at[1])
    near_copy.start()
    self_copy.start()
    products = Products(rank_ref, at_ref, x_ref, left_ref, right_ref, kept + rest, acc_ref)
    products.clear()
    for quarter in range(QUARTERS):
        sums = products.far(quarter * far_step, far_step)
        products.add(sums + products.near(kept_ref, quarter * kept_step, kept_step, 0))
    near_copy.wait()
    self_copy.wait()
    local_product(field_ref, shift_ref, self_ref, base_ref)
    products.add(products.near(near_ref, 0, rest, kept))
    finish(x_ref, acc_ref, field_ref, base_ref, out_ref)


def next_owner_kernel(
    rank_ref, at_ref, x_ref, near_ref, left_ref, right_ref, self_ref, field_ref, shift_ref, old_ref,
    out_ref, base_ref, steps_ref, acc_ref,
):
    near = near_ref.shape[0]
    near_step = near // QUARTERS
    far_step = left_ref.shape[0] // QUARTERS
    products = Products(rank_ref, at_ref, x_ref, left_ref, right_ref, near, acc_ref)
    products.clear()

    for quarter in range(QUARTERS):
        sums = products.far(quarter * far_step, far_step)
        if quarter == QUARTERS - 1:
            local_product(field_ref, shift_ref, self_ref, base_ref)
        products.add(sums + products.near(near_ref, quarter * near_step, near_step, 0))
    for step, (column, scale) in enumerate(factor(columns(old_ref[1]))):
        steps_ref[step] = column
        steps_ref[16, step : step + 1] = scale
    finish(x_ref, acc_ref, field_ref, base_ref, out_ref)


class Products:
    def __init__(self, rank_ref, at_ref, x_ref, left_ref, right_ref, near_count, acc_ref):
        self.rank_ref = rank_ref
        self.at_ref = at_ref
        self.x_ref = x_ref
        self.left_ref = left_ref
        self.right_ref = right_ref
        self.near_count = near_count
        self.acc_ref = acc_ref

    def clear(self):
        def some(at, carry):
            self.acc_ref[pl.ds(at * 8, 8)] = jnp.zeros((8, 16, 256), F32)
            return carry

        lax.fori_loop(0, self.acc_ref.shape[0] // 8, some, 0)

    def add(self, sums):
        for slot, value in sums:
            self.acc_ref[slot] += value

    def near(self, block_ref, first, count, shift):
        sums = []
        for part in range(count):
            which = first + part
            row, col = self.at_ref[0, shift + which], self.at_ref[1, shift + which]
            block = block_ref[which]
            sums.append(
                (row, lax.dot_general(self.x_ref[col], block, NT, preferred_element_type=F32))
            )
            sums.append((col, jnp.dot(self.x_ref[row], block, preferred_element_type=F32)))
        return sums

    def project(self, first):
        lane = iota((16, 256), 1)
        left = self.left_ref[pl.ds(first, 8)].reshape(256, 256)
        right = self.right_ref[pl.ds(first, 8)].reshape(256, 256)
        rows = [self.at_ref[0, self.near_count + first + part] for part in range(8)]
        cols = [self.at_ref[1, self.near_count + first + part] for part in range(8)]
        x_row = jnp.concatenate([self.x_ref[slot] for slot in rows], axis=0)
        x_col = jnp.concatenate([self.x_ref[slot] for slot in cols], axis=0)
        kept = jnp.concatenate(
            [
                (lane >= 32 * part) & (lane < 32 * part + self.rank_ref[first + part])
                for part in range(8)
            ],
            axis=0,
        )
        right_proj = lax.dot_general(x_col, right, NT, preferred_element_type=F32)
        left_proj = lax.dot_general(x_row, left, NT, preferred_element_type=F32)
        right_proj = jnp.where(kept, right_proj, 0.0).astype(BF16)
        left_proj = jnp.where(kept, left_proj, 0.0).astype(BF16)
        return rows, cols, left, right, right_proj, left_proj

    def far(self, first, count):
        sums = []
        for rows, cols, left, right, right_proj, left_proj in [
            self.project(first + at) for at in range(0, count, 8)
        ]:
            to_row = jnp.dot(right_proj, left, preferred_element_type=F32)
            to_col = jnp.dot(left_proj, right, preferred_element_type=F32)
            for part in range(8):
                sums.append((rows[part], to_row[16 * part : 16 * part + 16]))
                sums.append((cols[part], to_col[16 * part : 16 * part + 16]))
        return sums


def finish(x_ref, acc_ref, field_ref, base_ref, out_ref):
    slots = x_ref.shape[0]
    fields = field_ref[...].reshape(128, 256)
    curve = gram(fields, base_ref[...].reshape(128, 256))
    norm = gram(fields, fields)
    products = jnp.zeros((128, 128), F32)
    for at in range(slots // 16):
        here = slice(at * 16, at * 16 + 16)
        sums = acc_ref[here].astype(BF16)
        out_ref[here, 0:16, :] = sums[:, :, 0:128]
        out_ref[here, 16:32, :] = sums[:, :, 128:256]
        pair = lax.dot_general(
            x_ref[here].reshape(256, 256),
            sums.reshape(256, 256),
            NT,
            preferred_element_type=F32,
        )
        products = products + (pair[0:128, 0:128] + pair[128:256, 128:256])
    tile = pack(fold(products) + curve, norm)

    def attach(at, carry):
        out_ref[pl.ds(at * 8, 8), 32:40, :] = jnp.broadcast_to(tile[None], (8, 8, 128))
        return carry

    lax.fori_loop(0, slots // 8, attach, 0)


def add_returned(leaf_ref, sums_ref, accs):
    def some(at, tiles):
        for part in range(16):
            owner = at * 16 + part
            leaf = leaf_ref[owner]
            acc_ref = accs[part % len(accs)]
            acc_ref[leaf, :, 0:128] += sums_ref[owner, 0:16, :].astype(F32)
            acc_ref[leaf, :, 128:256] += sums_ref[owner, 16:32, :].astype(F32)
            tiles = tiles + sums_ref[owner, 32:40, :].astype(F32)
        return tiles

    for acc_ref in accs[1:]:
        acc_ref[...] = jnp.zeros(acc_ref.shape, F32)
    tiles = lax.fori_loop(0, sums_ref.shape[0] // 16, some, jnp.zeros((8, 128), F32))
    return tiles, (accs[0][...] + accs[1][...]) + (accs[2][...] + accs[3][...])


def leaf_kernel(
    leaf_ref, sums_ref, base_ref, field_ref,
    residual_ref, image_ref, small_ref, message_ref,
    half_ref, acc_a, acc_b, acc_c,
):
    image_ref[...] = base_ref[...]
    tiles, image = add_returned(leaf_ref, sums_ref, (image_ref, acc_a, acc_b, acc_c))
    curve, norm = unpack(tiles)
    step = solve(curve, norm)
    image_ref[...] = image
    image = image.reshape(128, 256)
    residual = field_ref[...].reshape(128, 256) - combine(image, kron_rows(step))
    half_ref[...] = residual.reshape(residual_ref.shape).astype(BF16)
    fill(leaf_ref, half_ref, message_ref)
    residual_ref[...] = residual.reshape(residual_ref.shape)
    small_ref[0] = from_columns(curve)
    small_ref[1] = norm
    small_ref[2] = step


def final_kernel(
    leaf_ref, sums_ref, base_ref, field_ref, residual_ref, image_ref, small_ref, steps_ref,
    solution_hbm, out_hbm, acc_ref, acc_a, acc_b, acc_c, solution_ref, out_ref, sems,
):
    acc_ref[...] = base_ref[...]
    tiles, returned = add_returned(leaf_ref, sums_ref, (acc_ref, acc_a, acc_b, acc_c))
    curve, next_norm = unpack(tiles)
    steps = [(steps_ref[step], steps_ref[16, step : step + 1]) for step in range(16)]
    coef = apply_factor(steps, next_norm)
    moved = product(columns(small_ref[0]), coef)
    moved = product(columns(coef.T[0:16]), moved)
    moved = columns(moved)
    step = solve([curve[at] - moved[at] for at in range(16)], next_norm)
    kron_coef = kron_rows(coef)
    part = combine_pieces(field_ref[...].reshape(128, 256), kron_rows(small_ref[2]))
    residual = residual_ref[...].reshape(128, 256)
    direction = residual + combine_pieces(field_ref[...].reshape(128, 256), kron_coef)
    image = returned.reshape(128, 256) + combine_pieces(
        image_ref[...].reshape(128, 256), kron_coef
    )
    kron_step = kron_rows(step)
    answer = part + combine_pieces(direction, kron_step)
    solution_ref[...] = answer.reshape(solution_ref.shape)
    solution_copy = pltpu.make_async_copy(solution_ref, solution_hbm, sems.at[0])
    solution_copy.start()
    out_ref[...] = (residual - combine_pieces(image, kron_step)).reshape(out_ref.shape)
    out_copy = pltpu.make_async_copy(out_ref, out_hbm, sems.at[1])
    out_copy.start()
    solution_copy.wait()
    out_copy.wait()


def call(kernel, ins, outs, scratch, cost=None):
    kinds = {pltpu.HBM: HBM, pltpu.SMEM: TABLE}
    spaces = [kinds.get(getattr(out, "memory_space", None), VMEM) for out in outs]
    run = pl.pallas_call(
        kernel,
        out_shape=list(outs),
        in_specs=list(ins),
        out_specs=spaces,
        scratch_shapes=list(scratch),
        compiler_params=pltpu.CompilerParams(vmem_limit_bytes=24 * 1024 * 1024),
        cost_estimate=cost,
    )

    def placed(*values):
        return run(
            *(
                pltpu.with_memory_space_constraint(value, spec.memory_space)
                if spec is not VMEM
                else value
                for value, spec in zip(values, ins)
            )
        )

    return placed


def swap(values):
    return lax.all_to_all(values, AXES, split_axis=0, concat_axis=0, tiled=True)


def shards(
    right_sides,
    diag_shift,
    self_blocks,
    near_blocks,
    far_left,
    far_right,
    far_rank,
    send_leaf,
    block_pos,
):
    leaves, rhs, size = right_sides.shape
    slots = send_leaf.shape[1]
    targets = send_leaf.reshape(slots)
    whole = (leaves, rhs, size)
    message = (slots, rhs, size)
    tables = [
        pltpu.SMEM((slots,), jnp.int32),
        pltpu.SMEM(far_rank.shape, jnp.int32),
        pltpu.SMEM(block_pos.shape, jnp.int32),
    ]
    send = call(
        send_kernel,
        [HBM, HBM, HBM, HBM, HBM],
        [jax.ShapeDtypeStruct(message, BF16)]
        + tables
        + [pltpu.VMEM((KEPT_NEAR, size, size), BF16)],
        [pltpu.VMEM(whole, F32), pltpu.VMEM(whole, BF16), pltpu.SemaphoreType.DMA((5,))],
    )
    owner_outs = [pltpu.VMEM((slots, 40, 128), BF16), pltpu.VMEM(whole, F32)]
    owner = call(
        first_owner_kernel,
        [TABLE, TABLE, VMEM, KEPT, HBM, VMEM, VMEM, HBM, VMEM, VMEM],
        owner_outs,
        [
            pltpu.VMEM((near_blocks.shape[0] - KEPT_NEAR, size, size), BF16),
            pltpu.VMEM(self_blocks.shape, BF16),
            pltpu.VMEM(message, F32),
            pltpu.SemaphoreType.DMA((2,)),
        ],
    )
    next_owner = call(
        next_owner_kernel,
        [TABLE, TABLE] + [VMEM] * 7 + [KEPT],
        owner_outs + [pltpu.VMEM((17, rhs, 128), F32)],
        [pltpu.VMEM(message, F32)],
    )
    leaf = call(
        leaf_kernel,
        [TABLE, VMEM, KEPT, VMEM],
        [
            pltpu.VMEM(whole, F32),
            pltpu.VMEM(whole, F32),
            pltpu.VMEM((3, rhs, 128), F32),
            jax.ShapeDtypeStruct(message, BF16),
        ],
        [pltpu.VMEM(whole, BF16)] + [pltpu.VMEM(whole, F32)] * 3,
    )
    final = call(
        final_kernel,
        [TABLE, VMEM, KEPT, VMEM, KEPT, KEPT, KEPT, KEPT],
        [pltpu.HBM(whole, F32), pltpu.HBM(whole, F32)],
        [pltpu.VMEM(whole, F32)] * 6 + [pltpu.SemaphoreType.DMA((2,))],
    )
    stored = (near_blocks, far_left, far_right, self_blocks)

    with jax.named_scope("send"):
        outgoing, leaf_table, rank_table, at_table, kept = send(
            targets, far_rank, block_pos, right_sides, near_blocks
        )
    incoming = swap(outgoing)
    with jax.named_scope("owner"):
        sums, base_image = owner(
            rank_table, at_table, incoming, kept, *stored, right_sides, diag_shift
        )
    back = swap(sums)
    with jax.named_scope("leaf"):
        residual, image, old, outgoing = leaf(leaf_table, back, base_image, right_sides)
    incoming = swap(outgoing)
    with jax.named_scope("owner"):
        sums, base_image, steps = next_owner(
            rank_table, at_table, incoming, *stored, residual, diag_shift, old
        )
    back = swap(sums)
    with jax.named_scope("final"):
        answer, residual = final(
            leaf_table, back, base_image, right_sides, residual, image, old, steps
        )
    return (answer, residual)


def solution(mesh):
    split = P(AXES, None, None)
    placed = (
        split,
        P(AXES, None),
        split,
        split,
        split,
        split,
        P(AXES),
        split,
        P(None, AXES),
    )
    return jax.shard_map(
        shards, mesh=mesh, in_specs=placed, out_specs=(split, split), check_vma=False
    )
```

```python
import jax
import jax.numpy as jnp
from jax import lax
from jax.experimental import pallas as pl
from jax.experimental.pallas import tpu as pltpu
from jax.sharding import PartitionSpec as P

AXES = ("clus", "grp")
KEPT_NEAR = 4
QUARTERS = 4
HIGHEST = lax.Precision.HIGHEST
NT = (((1,), (1,)), ((), ()))
F32 = jnp.float32
BF16 = jnp.bfloat16

VMEM = pl.BlockSpec(memory_space=pltpu.VMEM)
HBM = pl.BlockSpec(memory_space=pltpu.HBM)
KEPT = pl.BlockSpec(memory_space=pltpu.VMEM)
TABLE = pl.BlockSpec(memory_space=pltpu.SMEM)


def iota(shape, dim):
    return lax.broadcasted_iota(jnp.int32, shape, dim)


def spread(values):
    values = values + pltpu.roll(values, 64, 1)
    values = values + pltpu.roll(values, 32, 1)
    return values + pltpu.roll(values, 16, 1)


def block_mask():
    return iota((128, 128), 0) // 16 == iota((128, 128), 1) // 16


def fold(products):
    kept = jnp.where(block_mask(), products, 0.0)
    total = kept[0:16]
    for part in range(1, 8):
        total = total + kept[16 * part : 16 * part + 16]
    return spread(total)


def kron_rows(coefs):
    tiled = jnp.concatenate([coefs] * 8, axis=0)
    return jnp.where(block_mask(), tiled, 0.0).T


def combine(field, kron):
    return jnp.dot(kron, field, precision=HIGHEST, preferred_element_type=F32)


def pieces(values):
    high = values.astype(BF16)
    return high, (values - high.astype(F32)).astype(BF16)


def combine_pieces(field, kron):
    high, low = pieces(field)
    kron_high, kron_low = pieces(kron)
    main = jnp.dot(
        jnp.concatenate([kron_high, kron_low], axis=0), high, preferred_element_type=F32
    )
    rest = jnp.dot(kron_high, low, preferred_element_type=F32)
    return main[0:128] + (main[128:256] + rest)


def local_grams(field, image):
    high, low = pieces(field)
    image_high, image_low = pieces(image)
    main = lax.dot_general(
        jnp.concatenate([high, low], axis=0),
        jnp.concatenate([image_high, high], axis=0),
        NT,
        preferred_element_type=F32,
    )
    rest = lax.dot_general(
        high, jnp.concatenate([image_low, low], axis=0), NT, preferred_element_type=F32
    )
    both = main[0:128] + (main[128:256] + rest)
    return fold(both[:, 0:128]), fold(both[:, 128:256])


def columns(matrix):
    return [jnp.broadcast_to(matrix[:, at : at + 1], (16, 128)) for at in range(16)]


def factor(parts):
    row_at = iota((16, 128), 0)
    left = list(parts)
    steps = []
    for step in range(16):
        column = left[step]
        pivot = column[step : step + 1]
        scale = jnp.where(pivot > 0, 1.0 / pivot, jnp.nan)
        steps.append((column, scale))
        for later in range(step + 1, 16):
            scaled = left[later][step : step + 1] * scale
            left[later] = jnp.where(row_at == step, scaled, left[later] - column * scaled)
    return steps


def apply_factor(steps, target):
    row_at = iota((16, 128), 0)
    for step, (column, scale) in enumerate(steps):
        scaled = target[step : step + 1] * scale
        target = jnp.where(row_at == step, scaled, target - column * scaled)
    return target


def solve(parts, target):
    return apply_factor(factor(parts), target)


def product(left, right):
    total = left[0] * right[0:1]
    for at in range(1, 16):
        total = total + left[at] * right[at : at + 1]
    return total


def pack(first, second):
    group = iota((8, 128), 1) // 16
    tile = jnp.zeros((8, 128), F32)
    at = 0
    for matrix in (first, second):
        high = matrix.astype(BF16).astype(F32)
        low = matrix - high
        for piece in (high, low):
            for half in (piece[0:8], piece[8:16]):
                tile = jnp.where(group == at, half, tile)
                at += 1
    return tile.astype(BF16)


def unpack(tile):
    group = iota((8, 128), 1) // 16
    joined = tile + pltpu.roll(tile, 128 - 32, 1)
    first = [
        jnp.concatenate(
            [
                jnp.broadcast_to(joined[:, at : at + 1], (8, 128)),
                jnp.broadcast_to(joined[:, 16 + at : 17 + at], (8, 128)),
            ],
            axis=0,
        )
        for at in range(16)
    ]
    halves = [spread(jnp.where(group == at, joined, 0.0)) for at in (4, 5)]
    return first, jnp.concatenate(halves, axis=0)


def from_columns(parts):
    group = iota((16, 128), 1) % 16
    matrix = parts[0]
    for at in range(1, 16):
        matrix = jnp.where(group == at, parts[at], matrix)
    return matrix


def fill(leaf_ref, half_ref, message_ref):
    def some(at, carry):
        for inner in range(16):
            owner = at * 16 + inner
            message_ref[owner] = half_ref[leaf_ref[owner]]
        return carry

    lax.fori_loop(0, message_ref.shape[0] // 16, some, 0)


def send_kernel(
    leaf_hbm, rank_hbm, at_hbm, field_hbm, near_hbm,
    message_ref, leaf_ref, rank_ref, at_ref, kept_ref, field_ref, half_ref, sems,
):
    copies = [
        pltpu.make_async_copy(field_hbm, field_ref, sems.at[0]),
        pltpu.make_async_copy(leaf_hbm, leaf_ref, sems.at[1]),
        pltpu.make_async_copy(rank_hbm, rank_ref, sems.at[2]),
        pltpu.make_async_copy(at_hbm, at_ref, sems.at[3]),
        pltpu.make_async_copy(near_hbm.at[pl.ds(0, kept_ref.shape[0])], kept_ref, sems.at[4]),
    ]
    for copy in copies:
        copy.start()
    copies[0].wait()
    half_ref[...] = field_ref[...].astype(BF16)
    copies[1].wait()
    fill(leaf_ref, half_ref, message_ref)
    for copy in copies[2:]:
        copy.wait()


def local_product(field_ref, shift_ref, self_ref, base_ref):
    for leaf in range(field_ref.shape[0]):
        field = field_ref[leaf]
        half = field.astype(BF16)
        block = self_ref[leaf]
        total = shift_ref[leaf : leaf + 1, :] * field
        total = total + lax.dot_general(half, block, NT, preferred_element_type=F32)
        base_ref[leaf] = total + jnp.dot(half, block, preferred_element_type=F32)


def first_owner_kernel(
    rank_ref, at_ref, x_ref, kept_ref, near_hbm, left_ref, right_ref, self_hbm, field_ref, shift_ref,
    out_ref, base_ref, near_ref, self_ref, acc_ref, sems,
):
    kept = kept_ref.shape[0]
    kept_step = kept // QUARTERS
    far_step = left_ref.shape[0] // QUARTERS
    rest = near_ref.shape[0]
    near_copy = pltpu.make_async_copy(near_hbm.at[pl.ds(kept, rest)], near_ref, sems.at[0])
    self_copy = pltpu.make_async_copy(self_hbm, self_ref, sems.at[1])
    near_copy.start()
    self_copy.start()
    products = Products(rank_ref, at_ref, x_ref, left_ref, right_ref, kept + rest, acc_ref)
    products.clear()
    for quarter in range(QUARTERS):
        sums = products.far(quarter * far_step, far_step)
        products.add(sums + products.near(kept_ref, quarter * kept_step, kept_step, 0))
    near_copy.wait()
    self_copy.wait()
    local_product(field_ref, shift_ref, self_ref, base_ref)
    products.add(products.near(near_ref, 0, rest, kept))
    finish(x_ref, acc_ref, field_ref, base_ref, out_ref)


def next_owner_kernel(
    rank_ref, at_ref, x_ref, near_ref, left_ref, right_ref, self_ref, field_ref, shift_ref, old_ref,
    out_ref, base_ref, steps_ref, acc_ref,
):
    near = near_ref.shape[0]
    near_step = near // QUARTERS
    far_step = left_ref.shape[0] // QUARTERS
    products = Products(rank_ref, at_ref, x_ref, left_ref, right_ref, near, acc_ref)
    products.clear()

    for quarter in range(QUARTERS):
        sums = products.far(quarter * far_step, far_step)
        if quarter == QUARTERS - 1:
            local_product(field_ref, shift_ref, self_ref, base_ref)
        products.add(sums + products.near(near_ref, quarter * near_step, near_step, 0))
    for step, (column, scale) in enumerate(factor(columns(old_ref[1]))):
        steps_ref[step] = column
        steps_ref[16, step : step + 1] = scale
    finish(x_ref, acc_ref, field_ref, base_ref, out_ref)


class Products:
    def __init__(self, rank_ref, at_ref, x_ref, left_ref, right_ref, near_count, acc_ref):
        self.rank_ref = rank_ref
        self.at_ref = at_ref
        self.x_ref = x_ref
        self.left_ref = left_ref
        self.right_ref = right_ref
        self.near_count = near_count
        self.acc_ref = acc_ref

    def clear(self):
        def some(at, carry):
            self.acc_ref[pl.ds(at * 8, 8)] = jnp.zeros((8, 16, 256), F32)
            return carry

        lax.fori_loop(0, self.acc_ref.shape[0] // 8, some, 0)

    def add(self, sums):
        for slot, value in sums:
            self.acc_ref[slot] += value

    def near(self, block_ref, first, count, shift):
        sums = []
        for part in range(count):
            which = first + part
            row, col = self.at_ref[0, shift + which], self.at_ref[1, shift + which]
            block = block_ref[which]
            sums.append(
                (row, lax.dot_general(self.x_ref[col], block, NT, preferred_element_type=F32))
            )
            sums.append((col, jnp.dot(self.x_ref[row], block, preferred_element_type=F32)))
        return sums

    def project(self, first):
        lane = iota((16, 256), 1)
        left = self.left_ref[pl.ds(first, 8)].reshape(256, 256)
        right = self.right_ref[pl.ds(first, 8)].reshape(256, 256)
        rows = [self.at_ref[0, self.near_count + first + part] for part in range(8)]
        cols = [self.at_ref[1, self.near_count + first + part] for part in range(8)]
        x_row = jnp.concatenate([self.x_ref[slot] for slot in rows], axis=0)
        x_col = jnp.concatenate([self.x_ref[slot] for slot in cols], axis=0)
        kept = jnp.concatenate(
            [
                (lane >= 32 * part) & (lane < 32 * part + self.rank_ref[first + part])
                for part in range(8)
            ],
            axis=0,
        )
        right_proj = lax.dot_general(x_col, right, NT, preferred_element_type=F32)
        left_proj = lax.dot_general(x_row, left, NT, preferred_element_type=F32)
        right_proj = jnp.where(kept, right_proj, 0.0).astype(BF16)
        left_proj = jnp.where(kept, left_proj, 0.0).astype(BF16)
        return rows, cols, left, right, right_proj, left_proj

    def far(self, first, count):
        sums = []
        for rows, cols, left, right, right_proj, left_proj in [
            self.project(first + at) for at in range(0, count, 8)
        ]:
            to_row = jnp.dot(right_proj, left, preferred_element_type=F32)
            to_col = jnp.dot(left_proj, right, preferred_element_type=F32)
            for part in range(8):
                sums.append((rows[part], to_row[16 * part : 16 * part + 16]))
                sums.append((cols[part], to_col[16 * part : 16 * part + 16]))
        return sums


def finish(x_ref, acc_ref, field_ref, base_ref, out_ref):
    slots = x_ref.shape[0]
    fields = field_ref[...].reshape(128, 256)
    curve, norm = local_grams(fields, base_ref[...].reshape(128, 256))
    products = jnp.zeros((128, 128), F32)
    for at in range(slots // 16):
        here = slice(at * 16, at * 16 + 16)
        sums = acc_ref[here].astype(BF16)
        out_ref[here, 0:16, :] = sums[:, :, 0:128]
        out_ref[here, 16:32, :] = sums[:, :, 128:256]
        pair = lax.dot_general(
            x_ref[here].reshape(256, 256),
            sums.reshape(256, 256),
            NT,
            preferred_element_type=F32,
        )
        products = products + (pair[0:128, 0:128] + pair[128:256, 128:256])
    tile = pack(fold(products) + curve, norm)

    def attach(at, carry):
        out_ref[pl.ds(at * 8, 8), 32:40, :] = jnp.broadcast_to(tile[None], (8, 8, 128))
        return carry

    lax.fori_loop(0, slots // 8, attach, 0)


def add_returned(leaf_ref, sums_ref, accs):
    def some(at, tiles):
        for part in range(16):
            owner = at * 16 + part
            leaf = leaf_ref[owner]
            acc_ref = accs[part % len(accs)]
            acc_ref[leaf, :, 0:128] += sums_ref[owner, 0:16, :].astype(F32)
            acc_ref[leaf, :, 128:256] += sums_ref[owner, 16:32, :].astype(F32)
            tiles = tiles + sums_ref[owner, 32:40, :].astype(F32)
        return tiles

    for acc_ref in accs[1:]:
        acc_ref[...] = jnp.zeros(acc_ref.shape, F32)
    tiles = lax.fori_loop(0, sums_ref.shape[0] // 16, some, jnp.zeros((8, 128), F32))
    return tiles, (accs[0][...] + accs[1][...]) + (accs[2][...] + accs[3][...])


def leaf_kernel(
    leaf_ref, sums_ref, base_ref, field_ref,
    residual_ref, image_ref, small_ref, message_ref,
    half_ref, acc_a, acc_b, acc_c,
):
    image_ref[...] = base_ref[...]
    tiles, image = add_returned(leaf_ref, sums_ref, (image_ref, acc_a, acc_b, acc_c))
    curve, norm = unpack(tiles)
    step = solve(curve, norm)
    image_ref[...] = image
    image = image.reshape(128, 256)
    residual = field_ref[...].reshape(128, 256) - combine(image, kron_rows(step))
    half_ref[...] = residual.reshape(residual_ref.shape).astype(BF16)
    fill(leaf_ref, half_ref, message_ref)
    residual_ref[...] = residual.reshape(residual_ref.shape)
    small_ref[0] = from_columns(curve)
    small_ref[1] = norm
    small_ref[2] = step


def final_kernel(
    leaf_ref, sums_ref, base_ref, field_ref, residual_ref, image_ref, small_ref, steps_ref,
    solution_hbm, out_hbm, acc_ref, acc_a, acc_b, acc_c, solution_ref, out_ref, sems,
):
    acc_ref[...] = base_ref[...]
    tiles, returned = add_returned(leaf_ref, sums_ref, (acc_ref, acc_a, acc_b, acc_c))
    curve, next_norm = unpack(tiles)
    steps = [(steps_ref[step], steps_ref[16, step : step + 1]) for step in range(16)]
    coef = apply_factor(steps, next_norm)
    moved = product(columns(small_ref[0]), coef)
    moved = product(columns(coef.T[0:16]), moved)
    moved = columns(moved)
    step = solve([curve[at] - moved[at] for at in range(16)], next_norm)
    kron_coef = kron_rows(coef)
    part = combine_pieces(field_ref[...].reshape(128, 256), kron_rows(small_ref[2]))
    residual = residual_ref[...].reshape(128, 256)
    direction = residual + combine_pieces(field_ref[...].reshape(128, 256), kron_coef)
    image = returned.reshape(128, 256) + combine_pieces(
        image_ref[...].reshape(128, 256), kron_coef
    )
    kron_step = kron_rows(step)
    answer = part + combine_pieces(direction, kron_step)
    solution_ref[...] = answer.reshape(solution_ref.shape)
    solution_copy = pltpu.make_async_copy(solution_ref, solution_hbm, sems.at[0])
    solution_copy.start()
    out_ref[...] = (residual - combine_pieces(image, kron_step)).reshape(out_ref.shape)
    out_copy = pltpu.make_async_copy(out_ref, out_hbm, sems.at[1])
    out_copy.start()
    solution_copy.wait()
    out_copy.wait()


def call(kernel, ins, outs, scratch, cost=None):
    kinds = {pltpu.HBM: HBM, pltpu.SMEM: TABLE}
    spaces = [kinds.get(getattr(out, "memory_space", None), VMEM) for out in outs]
    run = pl.pallas_call(
        kernel,
        out_shape=list(outs),
        in_specs=list(ins),
        out_specs=spaces,
        scratch_shapes=list(scratch),
        compiler_params=pltpu.CompilerParams(vmem_limit_bytes=24 * 1024 * 1024),
        cost_estimate=cost,
    )

    def placed(*values):
        return run(
            *(
                pltpu.with_memory_space_constraint(value, spec.memory_space)
                if spec is not VMEM
                else value
                for value, spec in zip(values, ins)
            )
        )

    return placed


def swap(values):
    return lax.all_to_all(values, AXES, split_axis=0, concat_axis=0, tiled=True)


def shards(
    right_sides,
    diag_shift,
    self_blocks,
    near_blocks,
    far_left,
    far_right,
    far_rank,
    send_leaf,
    block_pos,
):
    leaves, rhs, size = right_sides.shape
    slots = send_leaf.shape[1]
    targets = send_leaf.reshape(slots)
    whole = (leaves, rhs, size)
    message = (slots, rhs, size)
    tables = [
        pltpu.SMEM((slots,), jnp.int32),
        pltpu.SMEM(far_rank.shape, jnp.int32),
        pltpu.SMEM(block_pos.shape, jnp.int32),
    ]
    send = call(
        send_kernel,
        [HBM, HBM, HBM, HBM, HBM],
        [jax.ShapeDtypeStruct(message, BF16)]
        + tables
        + [pltpu.VMEM((KEPT_NEAR, size, size), BF16)],
        [pltpu.VMEM(whole, F32), pltpu.VMEM(whole, BF16), pltpu.SemaphoreType.DMA((5,))],
    )
    owner_outs = [pltpu.VMEM((slots, 40, 128), BF16), pltpu.VMEM(whole, F32)]
    owner = call(
        first_owner_kernel,
        [TABLE, TABLE, VMEM, KEPT, HBM, VMEM, VMEM, HBM, VMEM, VMEM],
        owner_outs,
        [
            pltpu.VMEM((near_blocks.shape[0] - KEPT_NEAR, size, size), BF16),
            pltpu.VMEM(self_blocks.shape, BF16),
            pltpu.VMEM(message, F32),
            pltpu.SemaphoreType.DMA((2,)),
        ],
    )
    next_owner = call(
        next_owner_kernel,
        [TABLE, TABLE] + [VMEM] * 7 + [KEPT],
        owner_outs + [pltpu.VMEM((17, rhs, 128), F32)],
        [pltpu.VMEM(message, F32)],
    )
    leaf = call(
        leaf_kernel,
        [TABLE, VMEM, KEPT, VMEM],
        [
            pltpu.VMEM(whole, F32),
            pltpu.VMEM(whole, F32),
            pltpu.VMEM((3, rhs, 128), F32),
            jax.ShapeDtypeStruct(message, BF16),
        ],
        [pltpu.VMEM(whole, BF16)] + [pltpu.VMEM(whole, F32)] * 3,
    )
    final = call(
        final_kernel,
        [TABLE, VMEM, KEPT, VMEM, KEPT, KEPT, KEPT, KEPT],
        [pltpu.HBM(whole, F32), pltpu.HBM(whole, F32)],
        [pltpu.VMEM(whole, F32)] * 6 + [pltpu.SemaphoreType.DMA((2,))],
    )
    stored = (near_blocks, far_left, far_right, self_blocks)

    with jax.named_scope("send"):
        outgoing, leaf_table, rank_table, at_table, kept = send(
            targets, far_rank, block_pos, right_sides, near_blocks
        )
    incoming = swap(outgoing)
    with jax.named_scope("owner"):
        sums, base_image = owner(
            rank_table, at_table, incoming, kept, *stored, right_sides, diag_shift
        )
    back = swap(sums)
    with jax.named_scope("leaf"):
        residual, image, old, outgoing = leaf(leaf_table, back, base_image, right_sides)
    incoming = swap(outgoing)
    with jax.named_scope("owner"):
        sums, base_image, steps = next_owner(
            rank_table, at_table, incoming, *stored, residual, diag_shift, old
        )
    back = swap(sums)
    with jax.named_scope("final"):
        answer, residual = final(
            leaf_table, back, base_image, right_sides, residual, image, old, steps
        )
    return (answer, residual)


def solution(mesh):
    split = P(AXES, None, None)
    placed = (
        split,
        P(AXES, None),
        split,
        split,
        split,
        split,
        P(AXES),
        split,
        P(None, AXES),
    )
    return jax.shard_map(
        shards, mesh=mesh, in_specs=placed, out_specs=(split, split), check_vma=False
    )
```
